32 devices in a mesh: blk: 8 (over z, y), sec: 4 (over x, core).
Axes of the slice: x: 2, y: 2, z: 4, core: 2. Of those that a mesh axis runs over, the one named last changes fastest.
Arguments:
- factors: bfloat16 [8, 512, 1024], P('blk', None, 'sec'), may hold values from -0.5 to 0.5
- occ_energy: float32 [8], replicated, may hold values from -2 to -0.5
- vir_energy: float32 [512], replicated, may hold values from 0.2 to 3
- metric: float32 [1024, 1024], replicated, may hold values from -0.1875 to 0.1875
Outputs:
- gamma: float32 [1024, 8, 512], P('sec', 'blk')
- density: float32 [512, 512], P('blk')
The draws below stay inside these ranges and needn't reach their ends.
All inputs are finite; a program needn't handle non-finite values.
Results may differ from the reference program's by a relative error of at most 0.00077.
Values may be sent and summed in bfloat16 or wider, within the bound.
No kernel may reach another device: no remote copies, remote signals or barrier semaphores. Data moves between devices by JAX's collectives and lax.ppermute only.
A program may use at most 64 MiB of HBM per device.

```python
import jax
import jax.numpy as jnp
from jax import lax

V = 512
NAUX = 1024
OCC = 1
NO = 8
STEPS = 1
N_BLK = 8
N_SEC = 4


def block_levels(stream_key, extent, cuts, least, top_value):
    def one(axis_at, blocks):
        heights = jax.random.uniform(jax.random.fold_in(jax.random.fold_in(stream_key, 6), axis_at), (blocks,), jnp.float32, least / len(cuts), top_value / len(cuts))
        return jnp.repeat(jnp.exp(heights), extent[axis_at] // blocks).reshape((-1,) + (1,) * (len(extent) - axis_at - 1))

    factor_of = one(*cuts[0])
    for cut in cuts[1:]:
        factor_of = factor_of * one(*cut)
    return factor_of


def noise(own_key, shape, scale, reach, shards=(), dtype=jnp.bfloat16):
    values = scale * jax.random.normal(own_key, shape, jnp.float32)
    if shards:
        values = values * block_levels(own_key, shape, shards, -0.22, 0.18)
    return jnp.clip(values, -reach, reach).astype(dtype)


def setup_inputs(seed: int = 0) -> dict:
    arg_keys = jax.random.split(jax.random.key(seed), 5)
    factors = noise(arg_keys[0], (NO, V, NAUX), (V // 4) ** -0.5, 0.5, ((0, 8), (2, 4)))
    occ_energy = jnp.clip(jax.random.uniform(arg_keys[1], (NO,), jnp.float32, -2.0, -0.5), -2.0, -0.5)
    vir_energy = jnp.clip(jax.random.uniform(arg_keys[2], (V,), jnp.float32, 0.2, 3.0), 0.2, 3.0)
    metric = noise(arg_keys[3], (NAUX, NAUX), NAUX ** -0.5, 0.1875, (), jnp.float32)
    return dict(factors=factors, occ_energy=occ_energy, vir_energy=vir_energy, metric=metric)


def reference(factors, occ_energy, vir_energy, metric):
    window = STEPS * N_SEC
    orbitals = factors.shape[0]
    accumulated = jnp.zeros((orbitals, V, NAUX), jnp.float32)
    density = jnp.zeros((V, V), jnp.float32)
    total = N_BLK * window * OCC * OCC

    def one_pair(pair_index, loop_state):
        accumulated, density = loop_state
        first_pos = pair_index % OCC
        rest = pair_index // OCC
        second = rest % OCC
        rest = rest // OCC
        offset = rest % window
        batch_index = rest // window
        first_orb = (batch_index * OCC + first_pos).astype(jnp.int32)
        second_orb = (((batch_index - offset) % N_BLK) * OCC + second).astype(jnp.int32)
        left_block = lax.dynamic_index_in_dim(factors, first_orb, 0, keepdims=False).astype(jnp.float32)
        right_block = lax.dynamic_index_in_dim(factors, second_orb, 0, keepdims=False).astype(jnp.float32)
        intersection = jnp.dot(left_block, right_block.T, precision=lax.Precision.HIGHEST, preferred_element_type=jnp.float32)
        energy_sum = lax.dynamic_index_in_dim(occ_energy, first_orb, 0, keepdims=False) + lax.dynamic_index_in_dim(occ_energy, second_orb, 0, keepdims=False)
        denominator = energy_sum - vir_energy[:, None] - vir_energy[None, :]
        amplitude = intersection / denominator
        mixed_amp = 2.0 * amplitude - amplitude.T
        amp_half = lax.optimization_barrier(amplitude.astype(jnp.bfloat16)).astype(jnp.float32)
        mixed_half = lax.optimization_barrier(mixed_amp.astype(jnp.bfloat16)).astype(jnp.float32)
        weight = jnp.where(offset == 0, jnp.float32(0.5), jnp.float32(1.0))
        own_term = jnp.dot(mixed_half, right_block, precision=lax.Precision.HIGHEST, preferred_element_type=jnp.float32)
        part_term = jnp.dot(mixed_half.T, left_block, precision=lax.Precision.HIGHEST, preferred_element_type=jnp.float32)
        accumulated = accumulated.at[first_orb].add(weight * own_term)
        accumulated = accumulated.at[second_orb].add(weight * part_term)
        dens_term = jnp.dot(mixed_half, amp_half.T, precision=lax.Precision.HIGHEST, preferred_element_type=jnp.float32)
        dens_term = dens_term + jnp.dot(mixed_half.T, amp_half, precision=lax.Precision.HIGHEST, preferred_element_type=jnp.float32)
        density = density + weight * dens_term
        return accumulated, density

    accumulated, density = lax.fori_loop(0, total, one_pair, (accumulated, density))
    gamma = jnp.einsum("pq,iap->qia", metric.astype(jnp.float32), accumulated, precision=lax.Precision.HIGHEST)
    return gamma, density
```

```python
import jax
import jax.numpy as jnp
from jax import lax
from jax.experimental import pallas as pl
from jax.experimental.pallas import tpu as pltpu
from jax.sharding import PartitionSpec as P

CYCLE_STEPS = 4


def from_behind(shard, axis, by):
    devices = lax.axis_size(axis)
    return lax.ppermute(shard, axis, [(i, (i + by) % devices) for i in range(devices)])


def batch_energy(occ_energy, batch_index, per_batch):
    return lax.dynamic_slice_in_dim(occ_energy, batch_index * per_batch, per_batch, 0)


def pair_block(
    own_full, own_energy, partner, part_energy, vir_energy, acc_own, acc_part, density, weight
):
    per_batch = own_full.shape[0]

    def one_pair(pair_index, loop_state):
        acc_own, acc_part, density = loop_state
        first_pos = pair_index // per_batch
        second = pair_index % per_batch
        left_block = lax.dynamic_index_in_dim(own_full, first_pos, 0, keepdims=False)
        right_block = lax.dynamic_index_in_dim(partner, second, 0, keepdims=False)
        intersection = lax.dot_general(
            left_block, right_block, (((1,), (1,)), ((), ())), preferred_element_type=jnp.float32
        )
        energy_sum = lax.dynamic_index_in_dim(
            own_energy, first_pos, 0, keepdims=False
        ) + lax.dynamic_index_in_dim(part_energy, second, 0, keepdims=False)
        denominator = energy_sum - vir_energy[:, None] - vir_energy[None, :]
        amplitude = intersection / denominator
        mixed_amp = 2.0 * amplitude - amplitude.T
        amp_half = amplitude.astype(jnp.bfloat16)
        mixed_half = mixed_amp.astype(jnp.bfloat16)
        own_term = jnp.einsum(
            "bp,ab->pa", right_block, mixed_half, preferred_element_type=jnp.float32
        )
        acc_own = acc_own.at[first_pos].add(weight * own_term)
        dens_term = lax.dot_general(
            mixed_half, amp_half, (((1,), (1,)), ((), ())), preferred_element_type=jnp.float32
        )
        part_term = jnp.einsum(
            "ap,ab->pb", left_block, mixed_half, preferred_element_type=jnp.float32
        )
        acc_part = acc_part.at[second].add(weight * part_term)
        dens_term = dens_term + lax.dot_general(
            mixed_half, amp_half, (((0,), (0,)), ((), ())), preferred_element_type=jnp.float32
        )
        density = density + weight * dens_term
        return (acc_own, acc_part, density)

    return lax.fori_loop(0, per_batch * per_batch, one_pair, (acc_own, acc_part, density))


def general_device(factors, occ_energy, vir_energy, metric):
    n_blk = lax.axis_size("blk")
    n_sec = lax.axis_size("sec")
    blk_pos = lax.axis_index("blk")
    sec_pos = lax.axis_index("sec")
    per_batch = factors.shape[0]
    virtuals = factors.shape[1]
    aux_part = factors.shape[2]
    aux_total = aux_part * n_sec
    cycle_turns = min(CYCLE_STEPS, n_blk // (2 * n_sec))
    own_full = lax.all_gather(factors, "sec", axis=2, tiled=True)
    own_energy = batch_energy(occ_energy, blk_pos, per_batch)
    acc_own = jnp.zeros((per_batch, aux_total, virtuals), jnp.float32)
    density = jnp.zeros((virtuals, virtuals), jnp.float32)
    segmented = [factors]
    moving = factors
    for shift_turn in range(n_sec - 1):
        moving = from_behind(moving, "blk", 1)
        segmented.append(moving)
    partner = lax.all_to_all(
        jnp.stack(segmented, 0), "sec", split_axis=0, concat_axis=3, tiled=True
    )[0]
    acc_part = jnp.zeros((per_batch, aux_total, virtuals), jnp.float32)
    for cycle_step in range(cycle_turns):
        if cycle_step > 0:
            partner = from_behind(partner, "blk", n_sec)
            acc_part = from_behind(acc_part, "blk", n_sec)
        offset = sec_pos + n_sec * cycle_step
        weight = jnp.where(offset == 0, jnp.float32(0.5), jnp.float32(1.0))
        part_energy = batch_energy(occ_energy, (blk_pos - offset) % n_blk, per_batch)
        acc_own, acc_part, density = pair_block(
            own_full,
            own_energy,
            partner,
            part_energy,
            vir_energy,
            acc_own,
            acc_part,
            density,
            weight,
        )
    if cycle_turns > 1:
        acc_part = from_behind(acc_part, "blk", -n_sec * (cycle_turns - 1))
    regrouped = lax.all_to_all(acc_part[None], "sec", split_axis=2, concat_axis=0, tiled=True)
    carried = regrouped[n_sec - 1]
    for shift_turn in range(n_sec - 2, -1, -1):
        carried = from_behind(carried, "blk", -1) + regrouped[shift_turn]
    metric_rows = lax.dynamic_slice_in_dim(metric, sec_pos * aux_part, aux_part, 0)
    own_term = jnp.einsum("pq,ipa->qia", metric, acc_own, precision=lax.Precision.HIGHEST)
    gamma_part = lax.psum_scatter(
        own_term + jnp.einsum("pq,ipa->qia", metric_rows, carried, precision=lax.Precision.HIGHEST),
        "sec",
        scatter_dimension=0,
        tiled=True,
    )
    density_rows = lax.psum_scatter(density, "blk", scatter_dimension=0, tiled=True)
    density_out = lax.psum(density_rows, "sec")
    return (gamma_part, density_out)


AXES = ("blk", "sec")
NT = (((1,), (1,)), ((), ()))
NN = (((1,), (0,)), ((), ()))
TAIL_ROWS = 16
VMEM_LIMIT = 48 * 1024 * 1024


def dot(left, right, dims):
    return lax.dot_general(left, right, dims, preferred_element_type=jnp.float32)


def split_bits(device, n_sec):
    blk, sec = device // n_sec, device % n_sec
    return blk // 2, blk % 2, sec // 2, sec % 2


def join_bits(z, y, x, c, n_sec):
    return (2 * z + y) * n_sec + 2 * x + c


def send(value, target, n_blk, n_sec):
    pairs = []
    for device in range(n_blk * n_sec):
        pairs.append((device, join_bits(*target(*split_bits(device, n_sec)), n_sec)))
    return lax.ppermute(value, AXES, pairs)


def pair_terms(sum_energy, weight, row_energy, col_energy, left, right):
    straight = dot(left[0], right[0], NT)
    turned = dot(right[0], left[0], NT)
    for part in range(1, len(left)):
        straight += dot(left[part], right[part], NT)
        turned += dot(right[part], left[part], NT)
    amplitude = straight / (sum_energy - col_energy - row_energy)
    amplitude_t = turned / (sum_energy - row_energy - col_energy)
    mixed = (2.0 * amplitude - amplitude_t) * weight
    return amplitude.astype(jnp.bfloat16), mixed.astype(jnp.bfloat16)


def first_pair_kernel(scalars, row_energy, col_energy, *refs):
    left = [ref[...] for ref in refs[:4]]
    right = [ref[...] for ref in refs[4:8]]
    grad_out, dens_out = refs[8:]
    amp_half, mixed_half = pair_terms(
        scalars[0], scalars[1], row_energy[...], col_energy[...], left, right
    )
    width = right[0].shape[1]
    for part in range(4):
        grad_out[:, part * width : (part + 1) * width] = dot(mixed_half, right[part], NN)
    dens_out[...] = dot(mixed_half, amp_half, NT)


def last_pair_kernel(scalars, row_energy, col_energy, *refs):
    left = [ref[...] for ref in refs[:4]]
    right = [ref[...] for ref in refs[4:8]]
    grad_in, dens_in, high_out, low_out, dens_out = refs[8:]
    amp_half, mixed_half = pair_terms(
        scalars[0], scalars[1], row_energy[...], col_energy[...], left, right
    )
    width = right[0].shape[1]
    for part in range(4):
        cols = slice(part * width, (part + 1) * width)
        grad = grad_in[:, cols] + dot(mixed_half, right[part], NN)
        high = grad.astype(jnp.bfloat16)
        high_out[:, cols] = high
        low_out[:, cols] = (grad - high.astype(jnp.float32)).astype(jnp.bfloat16)
    dens_out[...] = dens_in[...] + dot(mixed_half, amp_half, NT)


def metric_kernel(metric_high, metric_low, high, low, out, peak):
    metric_top = metric_high[0]
    block = dot(metric_top, high[...], NT)
    block += dot(metric_top, low[...], NT)
    block += dot(metric_low[0], high[...], NT)
    out[...] = block
    peak[...] = jnp.max(jnp.abs(block), keepdims=True)


def turn_metric_kernel(order, metric, high, low):
    turned = metric[...].T
    top = turned.astype(jnp.bfloat16)
    high[0] = top
    low[0] = (turned - top.astype(jnp.float32)).astype(jnp.bfloat16)


def pack16(value, peak):
    power = jnp.clip(jnp.floor(14.0 - jnp.log2(jnp.maximum(peak, 1e-30))), -110.0, 110.0)
    scaled = (value * jnp.exp2(power)).astype(jnp.float16)
    tail = jnp.broadcast_to(power.astype(jnp.float16), (TAIL_ROWS, value.shape[1]))
    return jnp.concatenate([scaled, tail], 0)


def unpack16(packed):
    rows = packed.shape[0] - TAIL_ROWS
    power = packed[rows, 0].astype(jnp.float32)
    return packed[:rows].astype(jnp.float32) * jnp.exp2(-power)


def fast_device(factors, occ_energy, vir_energy, metric):
    n_blk = lax.axis_size("blk")
    n_sec = lax.axis_size("sec")
    blk_pos = lax.axis_index("blk")
    sec_pos = lax.axis_index("sec")
    z, y = blk_pos // 2, blk_pos % 2
    x, c = sec_pos // 2, sec_pos % 2
    n_lay = n_blk // 2
    half_lay = n_lay // 2
    own = factors[0]
    virtuals, width = own.shape
    aux_total = width * n_sec

    def move(value, target):
        return send(value, target, n_blk, n_sec)

    def core_swap(value):
        return move(value, lambda z, y, x, c: (z, y, x, 1 - c))

    def x_swap(value):
        return move(value, lambda z, y, x, c: (z, y, 1 - x, c))

    def y_swap(value):
        return move(value, lambda z, y, x, c: (z, 1 - y, x, c))

    def first_partner(value):
        return move(value, lambda z, y, x, c: (z if x else z ^ 1, y, x, c))

    def last_partner(value):
        return move(value, lambda z, y, x, c: (z ^ 3 if x else z ^ 2, y, x, c))

    with jax.named_scope("gather"):
        swapped = x_swap(own)
        last_own = last_partner(own)
        first_own = first_partner(own)
        other_own = y_swap(own)
        last_swapped = last_partner(swapped)
        first_swapped = first_partner(swapped)
        other_swapped = y_swap(swapped)
        at_home = c == y
        left_mine = [
            jnp.where(at_home, own, other_own),
            jnp.where(at_home, swapped, other_swapped),
        ]
        left_sent = jnp.stack(
            [
                jnp.where(at_home, other_own, own),
                jnp.where(at_home, other_swapped, swapped),
            ],
            0,
        )
        left_got = core_swap(left_sent)
        left = left_mine + [left_got[0], left_got[1]]
        first = [first_own, first_swapped, core_swap(first_own), core_swap(first_swapped)]
        last = [last_own, last_swapped, core_swap(last_own), core_swap(last_swapped)]

    home_energy = lax.dynamic_index_in_dim(occ_energy, 2 * z + c, 0, keepdims=False)

    def energy_of(layer):
        return lax.dynamic_index_in_dim(occ_energy, 2 * layer + y, 0, keepdims=False)

    first_layer = jnp.where(x == 1, z, z ^ 1)
    last_layer = jnp.where(x == 1, z ^ 3, z ^ 2)
    first_scalars = jnp.stack([home_energy + energy_of(first_layer), jnp.float32(1.0)])
    last_weight = jnp.where((x == 0) & (c == y), jnp.float32(0.0), jnp.float32(1.0))
    last_scalars = jnp.stack([home_energy + energy_of(last_layer), last_weight])
    row_energy, col_energy = vir_energy[None, :], vir_energy[:, None]

    smem = pl.BlockSpec(memory_space=pltpu.SMEM)
    vmem = pl.BlockSpec(memory_space=pltpu.VMEM)
    params = pltpu.CompilerParams(vmem_limit_bytes=VMEM_LIMIT)
    square = 2 * virtuals * virtuals
    grad_shape = (virtuals, aux_total)

    def blocks_of_round(step):
        return 2 * (x ^ (step >> 1)) + (y ^ (step & 1))

    with jax.named_scope("metric_turn"):
        order = jnp.stack(
            [sec_pos, sec_pos ^ 2, sec_pos ^ 1, sec_pos ^ 3]
            + [blocks_of_round(step) for step in range(4)]
        ).astype(jnp.int32)
        turned = jax.ShapeDtypeStruct((4, width, aux_total), jnp.bfloat16)
        turned_spec = pl.BlockSpec((1, width, width), lambda r, k, order: (r, 0, k))
        metric_high, metric_low = pl.pallas_call(
            turn_metric_kernel,
            grid_spec=pltpu.PrefetchScalarGridSpec(
                num_scalar_prefetch=1,
                grid=(4, 4),
                in_specs=[
                    pl.BlockSpec((width, width), lambda r, k, order: (order[k], order[4 + r]))
                ],
                out_specs=[turned_spec, turned_spec],
            ),
            out_shape=[turned, turned],
        )(order, metric)

    with jax.named_scope("first_pair"):
        grad, dens = pl.pallas_call(
            first_pair_kernel,
            in_specs=[smem] + [vmem] * 10,
            out_specs=[vmem, vmem],
            out_shape=[
                jax.ShapeDtypeStruct(grad_shape, jnp.float32),
                jax.ShapeDtypeStruct((virtuals, virtuals), jnp.float32),
            ],
            compiler_params=params,
            cost_estimate=pl.CostEstimate(
                flops=square * (3 * aux_total + virtuals),
                bytes_accessed=10 * virtuals * aux_total,
                transcendentals=0,
            ),
        )(first_scalars, row_energy, col_energy, *left, *first)

    with jax.named_scope("last_pair"):
        high, low, dens = pl.pallas_call(
            last_pair_kernel,
            in_specs=[smem] + [vmem] * 12,
            out_specs=[vmem] * 3,
            out_shape=[
                jax.ShapeDtypeStruct(grad_shape, jnp.bfloat16),
                jax.ShapeDtypeStruct(grad_shape, jnp.bfloat16),
                jax.ShapeDtypeStruct((virtuals, virtuals), jnp.float32),
            ],
            compiler_params=params,
            cost_estimate=pl.CostEstimate(
                flops=square * (3 * aux_total + virtuals),
                bytes_accessed=16 * virtuals * aux_total,
                transcendentals=0,
            ),
        )(last_scalars, row_energy, col_energy, *left, *last, grad, dens)

    with jax.named_scope("gamma"):
        got = []
        for step in range(4):
            metric_spec = pl.BlockSpec((1, width, aux_total), lambda i, step=step: (step, 0, 0))
            whole = pl.BlockSpec(grad_shape, lambda i: (0, 0))
            block, peak = pl.pallas_call(
                metric_kernel,
                grid=(1,),
                in_specs=[metric_spec, metric_spec, whole, whole],
                out_specs=[
                    pl.BlockSpec((width, virtuals), lambda i: (0, 0)),
                    pl.BlockSpec((1, 1), lambda i: (0, 0)),
                ],
                out_shape=[
                    jax.ShapeDtypeStruct((width, virtuals), jnp.float32),
                    jax.ShapeDtypeStruct((1, 1), jnp.float32),
                ],
                compiler_params=params,
                cost_estimate=pl.CostEstimate(
                    flops=6 * width * virtuals * aux_total,
                    bytes_accessed=4 * (width + virtuals) * aux_total,
                    transcendentals=0,
                ),
            )(metric_high, metric_low, high, low)
            packed = pack16(block, peak)
            got.append(
                move(
                    packed,
                    lambda z, y, x, c, step=step: (z, c, x ^ (step >> 1), y ^ (step & 1)),
                )
            )
        total = unpack16(got[0])
        for packed in got[1:]:
            total = total + unpack16(packed)
        gamma = total[:, None, :]

    with jax.named_scope("density"):
        half = virtuals // 2
        layer_rows = virtuals // n_lay
        rows = virtuals // n_blk
        got_half = core_swap(lax.dynamic_slice_in_dim(dens, (1 - c) * half, half, 1))
        dens = lax.dynamic_slice_in_dim(dens, c * half, half, 1) + got_half
        dens = dens.reshape(n_lay, layer_rows, half)
        peak = jnp.max(jnp.abs(dens))
        layer = lax.dynamic_index_in_dim(dens, z, 0, keepdims=False)
        for step in range(1, n_lay):
            packed = pack16(lax.dynamic_index_in_dim(dens, z ^ step, 0, keepdims=False), peak)
            layer = layer + unpack16(
                move(packed, lambda z, y, x, c, step=step: (z ^ step, y, x, c))
            )
        mine = lax.dynamic_slice_in_dim(layer, y * rows, rows, 0)
        theirs = lax.dynamic_slice_in_dim(layer, (1 - y) * rows, rows, 0)
        from_y = y_swap(theirs)
        from_xy = move(theirs, lambda z, y, x, c: (z, 1 - y, 1 - x, c))
        block = (mine + x_swap(mine)) + (from_y + from_xy)
        other = core_swap(block)
        density = jnp.where(
            c == 0,
            jnp.concatenate([block, other], 1),
            jnp.concatenate([other, block], 1),
        )
    return gamma, density


def solution(mesh):
    n_blk, n_sec = mesh.shape["blk"], mesh.shape["sec"]

    def per_device(factors, occ_energy, vir_energy, metric):
        two_rows_of_layers = n_sec == 4 and n_blk == 2 * n_sec and factors.shape[0] == 1
        step = fast_device if two_rows_of_layers else general_device
        return step(factors, occ_energy, vir_energy, metric)

    return jax.shard_map(
        per_device,
        mesh=mesh,
        in_specs=(P("blk", None, "sec"), P(), P(), P()),
        out_specs=(P("sec", "blk", None), P("blk", None)),
        check_vma=False,
    )
```

```python
import jax
import jax.numpy as jnp
from jax import lax
from jax.experimental import pallas as pl
from jax.experimental.pallas import tpu as pltpu
from jax.sharding import PartitionSpec as P

CYCLE_STEPS = 4


def from_behind(shard, axis, by):
    devices = lax.axis_size(axis)
    return lax.ppermute(shard, axis, [(i, (i + by) % devices) for i in range(devices)])


def batch_energy(occ_energy, batch_index, per_batch):
    return lax.dynamic_slice_in_dim(occ_energy, batch_index * per_batch, per_batch, 0)


def pair_block(
    own_full, own_energy, partner, part_energy, vir_energy, acc_own, acc_part, density, weight
):
    per_batch = own_full.shape[0]

    def one_pair(pair_index, loop_state):
        acc_own, acc_part, density = loop_state
        first_pos = pair_index // per_batch
        second = pair_index % per_batch
        left_block = lax.dynamic_index_in_dim(own_full, first_pos, 0, keepdims=False)
        right_block = lax.dynamic_index_in_dim(partner, second, 0, keepdims=False)
        intersection = lax.dot_general(
            left_block, right_block, (((1,), (1,)), ((), ())), preferred_element_type=jnp.float32
        )
        energy_sum = lax.dynamic_index_in_dim(
            own_energy, first_pos, 0, keepdims=False
        ) + lax.dynamic_index_in_dim(part_energy, second, 0, keepdims=False)
        denominator = energy_sum - vir_energy[:, None] - vir_energy[None, :]
        amplitude = intersection / denominator
        mixed_amp = 2.0 * amplitude - amplitude.T
        amp_half = amplitude.astype(jnp.bfloat16)
        mixed_half = mixed_amp.astype(jnp.bfloat16)
        own_term = jnp.einsum(
            "bp,ab->pa", right_block, mixed_half, preferred_element_type=jnp.float32
        )
        acc_own = acc_own.at[first_pos].add(weight * own_term)
        dens_term = lax.dot_general(
            mixed_half, amp_half, (((1,), (1,)), ((), ())), preferred_element_type=jnp.float32
        )
        part_term = jnp.einsum(
            "ap,ab->pb", left_block, mixed_half, preferred_element_type=jnp.float32
        )
        acc_part = acc_part.at[second].add(weight * part_term)
        dens_term = dens_term + lax.dot_general(
            mixed_half, amp_half, (((0,), (0,)), ((), ())), preferred_element_type=jnp.float32
        )
        density = density + weight * dens_term
        return (acc_own, acc_part, density)

    return lax.fori_loop(0, per_batch * per_batch, one_pair, (acc_own, acc_part, density))


def general_device(factors, occ_energy, vir_energy, metric):
    n_blk = lax.axis_size("blk")
    n_sec = lax.axis_size("sec")
    blk_pos = lax.axis_index("blk")
    sec_pos = lax.axis_index("sec")
    per_batch = factors.shape[0]
    virtuals = factors.shape[1]
    aux_part = factors.shape[2]
    aux_total = aux_part * n_sec
    cycle_turns = min(CYCLE_STEPS, n_blk // (2 * n_sec))
    own_full = lax.all_gather(factors, "sec", axis=2, tiled=True)
    own_energy = batch_energy(occ_energy, blk_pos, per_batch)
    acc_own = jnp.zeros((per_batch, aux_total, virtuals), jnp.float32)
    density = jnp.zeros((virtuals, virtuals), jnp.float32)
    segmented = [factors]
    moving = factors
    for shift_turn in range(n_sec - 1):
        moving = from_behind(moving, "blk", 1)
        segmented.append(moving)
    partner = lax.all_to_all(
        jnp.stack(segmented, 0), "sec", split_axis=0, concat_axis=3, tiled=True
    )[0]
    acc_part = jnp.zeros((per_batch, aux_total, virtuals), jnp.float32)
    for cycle_step in range(cycle_turns):
        if cycle_step > 0:
            partner = from_behind(partner, "blk", n_sec)
            acc_part = from_behind(acc_part, "blk", n_sec)
        offset = sec_pos + n_sec * cycle_step
        weight = jnp.where(offset == 0, jnp.float32(0.5), jnp.float32(1.0))
        part_energy = batch_energy(occ_energy, (blk_pos - offset) % n_blk, per_batch)
        acc_own, acc_part, density = pair_block(
            own_full,
            own_energy,
            partner,
            part_energy,
            vir_energy,
            acc_own,
            acc_part,
            density,
            weight,
        )
    if cycle_turns > 1:
        acc_part = from_behind(acc_part, "blk", -n_sec * (cycle_turns - 1))
    regrouped = lax.all_to_all(acc_part[None], "sec", split_axis=2, concat_axis=0, tiled=True)
    carried = regrouped[n_sec - 1]
    for shift_turn in range(n_sec - 2, -1, -1):
        carried = from_behind(carried, "blk", -1) + regrouped[shift_turn]
    metric_rows = lax.dynamic_slice_in_dim(metric, sec_pos * aux_part, aux_part, 0)
    own_term = jnp.einsum("pq,ipa->qia", metric, acc_own, precision=lax.Precision.HIGHEST)
    gamma_part = lax.psum_scatter(
        own_term + jnp.einsum("pq,ipa->qia", metric_rows, carried, precision=lax.Precision.HIGHEST),
        "sec",
        scatter_dimension=0,
        tiled=True,
    )
    density_rows = lax.psum_scatter(density, "blk", scatter_dimension=0, tiled=True)
    density_out = lax.psum(density_rows, "sec")
    return (gamma_part, density_out)


AXES = ("blk", "sec")
NT = (((1,), (1,)), ((), ()))
NN = (((1,), (0,)), ((), ()))
TAIL_ROWS = 16
VMEM_LIMIT = 20 * 1024 * 1024


def dot(left, right, dims):
    return lax.dot_general(left, right, dims, preferred_element_type=jnp.float32)


def split_bits(device, n_sec):
    blk, sec = device // n_sec, device % n_sec
    return blk // 2, blk % 2, sec // 2, sec % 2


def join_bits(z, y, x, c, n_sec):
    return (2 * z + y) * n_sec + 2 * x + c


def send(value, target, n_blk, n_sec):
    pairs = []
    for device in range(n_blk * n_sec):
        pairs.append((device, join_bits(*target(*split_bits(device, n_sec)), n_sec)))
    return lax.ppermute(value, AXES, pairs)


def encode(value):
    peak = jnp.max(jnp.abs(value), keepdims=True)
    power = jnp.floor(15.4 - jnp.log2(jnp.maximum(peak, 1e-36)))
    power = jnp.clip(power, -120.0, 120.0)
    scaled = value * jnp.exp2(power)
    second = scaled * scaled
    fourth = second * second
    eighth = fourth * fourth
    coded = jnp.where(scaled < 0.0, -eighth, eighth).astype(jnp.bfloat16)
    tail = jnp.broadcast_to(power, (TAIL_ROWS, value.shape[1])).astype(jnp.bfloat16)
    return coded, tail


def encode_into(out, value):
    rows = value.shape[0]
    coded, tail = encode(value)
    out[:rows] = coded
    out[rows:] = tail


def decode(ref):
    rows = ref.shape[0] - TAIL_ROWS
    power = ref[rows:].astype(jnp.float32)[:1]
    coded = ref[:rows].astype(jnp.float32)
    root = jnp.sqrt(jnp.sqrt(jnp.sqrt(jnp.abs(coded)))) * jnp.exp2(-power)
    return jnp.where(coded < 0.0, -root, root)


def pair_terms(sum_energy, weight, row_energy, col_energy, left, right):
    straight = dot(left[0], right[0], NT)
    turned = dot(right[0], left[0], NT)
    for part in range(1, len(left)):
        straight += dot(left[part], right[part], NT)
        turned += dot(right[part], left[part], NT)
    amplitude = straight / (sum_energy - col_energy - row_energy)
    amplitude_t = turned / (sum_energy - row_energy - col_energy)
    mixed = (2.0 * amplitude - amplitude_t) * weight
    return amplitude.astype(jnp.bfloat16), mixed.astype(jnp.bfloat16)


def first_pair_kernel(scalars, row_energy, col_energy, *refs):
    left = [ref[...] for ref in refs[:4]]
    right = [ref[...] for ref in refs[4:8]]
    grad_out, amp_out, mixed_out = refs[8:]
    amp_half, mixed_half = pair_terms(
        scalars[0], scalars[1], row_energy[...], col_energy[...], left, right
    )
    width = right[0].shape[1]
    for part in range(4):
        grad_out[:, part * width : (part + 1) * width] = dot(mixed_half, right[part], NN)
    amp_out[...] = amp_half
    mixed_out[...] = mixed_half


def last_pair_kernel(place, scalars, row_energy, col_energy, *refs):
    left = [ref[...] for ref in refs[:4]]
    right = [ref[...] for ref in refs[4:8]]
    grad_in, first_amp, first_mixed = refs[8:11]
    high_out, low_out, dens_keep, dens_send, amp = refs[11:]
    amp_half, mixed_half = pair_terms(
        scalars[0], scalars[1], row_energy[...], col_energy[...], left, right
    )
    amp[...] = amp_half
    half = amp.shape[0] // 2
    mixed_first = first_mixed[...]
    for out, core in ((dens_send, 1 - place[0]), (dens_keep, place[0])):
        rows = pl.ds(pl.multiple_of(core * half, half), half)
        out[...] = dot(mixed_half, amp[rows, :], NT) + dot(mixed_first, first_amp[rows, :], NT)
    width = right[0].shape[1]
    for part in range(4):
        cols = slice(part * width, (part + 1) * width)
        grad = grad_in[:, cols] + dot(mixed_half, right[part], NN)
        high = grad.astype(jnp.bfloat16)
        high_out[:, cols] = high
        low_out[:, cols] = (grad - high.astype(jnp.float32)).astype(jnp.bfloat16)


def metric_kernel(metric_high, metric_low, high, low, out):
    metric_top = metric_high[0]
    block = dot(metric_top, high[...], NT)
    block += dot(metric_top, low[...], NT)
    block += dot(metric_low[0], high[...], NT)
    encode_into(out, block)


def turn_metric_kernel(order, metric, high, low):
    width = metric.shape[1]
    row = lax.broadcasted_iota(jnp.int32, (width, width), 0)
    col = lax.broadcasted_iota(jnp.int32, (width, width), 1)
    unit = jnp.where(row == col, 1.0, 0.0).astype(jnp.bfloat16)
    for part in range(metric.shape[0] // width):
        rows = pl.ds(pl.multiple_of(order[part] * width, width), width)
        cols = slice(part * width, (part + 1) * width)
        value = metric[rows, :]
        top = value.astype(jnp.bfloat16)
        rest = (value - top.astype(jnp.float32)).astype(jnp.bfloat16)
        high[0, :, cols] = dot(unit, top, NT).astype(jnp.bfloat16)
        low[0, :, cols] = dot(unit, rest, NT).astype(jnp.bfloat16)


def gamma_sum_kernel(*refs):
    out = refs[-1]
    total = decode(refs[0])
    for ref in refs[1:-1]:
        total += decode(ref)
    out[:, 0, :] = total


def density_layers_kernel(place, keep, got, layer, *outs):
    rows = layer.shape[0]
    here = pl.ds(pl.multiple_of(place[1] * rows, rows), rows)
    layer[...] = keep[here, :] + got[here, :]
    for step, out in enumerate(outs, 1):
        there = pl.ds(pl.multiple_of((place[1] ^ step) * rows, rows), rows)
        encode_into(out, keep[there, :] + got[there, :])


def density_rows_kernel(place, layer, *refs):
    mine, theirs, total = refs[-3:]
    value = layer[...]
    for ref in refs[:-3]:
        value += decode(ref)
    total[...] = value
    rows = mine.shape[0]
    mine[...] = total[pl.ds(pl.multiple_of(place[2] * rows, rows), rows), :]
    theirs[...] = total[pl.ds(pl.multiple_of((1 - place[2]) * rows, rows), rows), :]


def fast_device(factors, occ_energy, vir_energy, metric):
    n_blk = lax.axis_size("blk")
    n_sec = lax.axis_size("sec")
    blk_pos = lax.axis_index("blk")
    sec_pos = lax.axis_index("sec")
    z, y = blk_pos // 2, blk_pos % 2
    x, c = sec_pos // 2, sec_pos % 2
    n_lay = n_blk // 2
    own = factors[0]
    virtuals, width = own.shape
    aux_total = width * n_sec
    half = virtuals // 2
    place = jnp.stack([c, z, y]).astype(jnp.int32)

    def move(value, target):
        return send(value, target, n_blk, n_sec)

    def core_swap(value):
        return move(value, lambda z, y, x, c: (z, y, x, 1 - c))

    def x_swap(value):
        return move(value, lambda z, y, x, c: (z, y, 1 - x, c))

    def y_swap(value):
        return move(value, lambda z, y, x, c: (z, 1 - y, x, c))

    def xy_swap(value):
        return move(value, lambda z, y, x, c: (z, 1 - y, 1 - x, c))

    def first_partner(value):
        return move(value, lambda z, y, x, c: (z if x else z ^ 1, y, x, c))

    def last_partner(value):
        return move(value, lambda z, y, x, c: (z ^ 3 if x else z ^ 2, y, x, c))

    smem = pl.BlockSpec(memory_space=pltpu.SMEM)
    vmem = pl.BlockSpec(memory_space=pltpu.VMEM)
    params = pltpu.CompilerParams(vmem_limit_bytes=VMEM_LIMIT)
    square = 2 * virtuals * virtuals
    grad_shape = (virtuals, aux_total)

    def cost(flops, size):
        return pl.CostEstimate(flops=flops, bytes_accessed=size, transcendentals=0)

    def shape(rows, cols, dtype):
        return jax.ShapeDtypeStruct((rows, cols), dtype)

    with jax.named_scope("metric_turn"):
        order = jnp.stack(
            [sec_pos, sec_pos ^ 2, sec_pos ^ 1, sec_pos ^ 3]
            + [2 * (x ^ (step >> 1)) + (y ^ (step & 1)) for step in range(4)]
        ).astype(jnp.int32)
        turned = jax.ShapeDtypeStruct((4, width, aux_total), jnp.bfloat16)
        turned_spec = pl.BlockSpec((1, width, aux_total), lambda r, order: (r, 0, 0))
        metric_high, metric_low = pl.pallas_call(
            turn_metric_kernel,
            grid_spec=pltpu.PrefetchScalarGridSpec(
                num_scalar_prefetch=1,
                grid=(4,),
                in_specs=[pl.BlockSpec((aux_total, width), lambda r, order: (0, order[4 + r]))],
                out_specs=[turned_spec, turned_spec],
            ),
            out_shape=[turned, turned],
            cost_estimate=cost(4 * aux_total * aux_total * width, 8 * aux_total**2),
        )(order, metric)

    with jax.named_scope("gather"):
        last_own = last_partner(own)
        swapped = x_swap(own)
        first_own = first_partner(own)
        other_own = y_swap(own)
        other_swapped = xy_swap(own)
        swapped, other_own, other_swapped, first_own, last_own, metric_high, metric_low = (
            lax.optimization_barrier(
                (
                    swapped,
                    other_own,
                    other_swapped,
                    first_own,
                    last_own,
                    metric_high,
                    metric_low,
                )
            )
        )
        last_swapped = last_partner(swapped)
        first_swapped = first_partner(swapped)
        first_own_other = core_swap(first_own)
        last_own_other = core_swap(last_own)
        at_home = c == y
        left_mine = [
            jnp.where(at_home, own, other_own),
            jnp.where(at_home, swapped, other_swapped),
        ]
        left_sent = [
            jnp.where(at_home, other_own, own),
            jnp.where(at_home, other_swapped, swapped),
        ]
        left = left_mine + [core_swap(left_sent[0]), core_swap(left_sent[1])]
        first = [first_own, first_swapped, first_own_other, core_swap(first_swapped)]
        last = [last_own, last_swapped, last_own_other, core_swap(last_swapped)]

    home_energy = lax.dynamic_index_in_dim(occ_energy, 2 * z + c, 0, keepdims=False)

    def energy_of(layer):
        return lax.dynamic_index_in_dim(occ_energy, 2 * layer + y, 0, keepdims=False)

    first_layer = jnp.where(x == 1, z, z ^ 1)
    last_layer = jnp.where(x == 1, z ^ 3, z ^ 2)
    first_scalars = jnp.stack([home_energy + energy_of(first_layer), jnp.float32(1.0)])
    last_weight = jnp.where((x == 0) & (c == y), jnp.float32(0.0), jnp.float32(1.0))
    last_scalars = jnp.stack([home_energy + energy_of(last_layer), last_weight])
    row_energy, col_energy = vir_energy[None, :], vir_energy[:, None]

    with jax.named_scope("first_pair"):
        grad, first_amp, first_mixed = pl.pallas_call(
            first_pair_kernel,
            in_specs=[smem] + [vmem] * 10,
            out_specs=[vmem] * 3,
            out_shape=[
                shape(virtuals, aux_total, jnp.float32),
                shape(virtuals, virtuals, jnp.bfloat16),
                shape(virtuals, virtuals, jnp.bfloat16),
            ],
            compiler_params=params,
            cost_estimate=cost(3 * square * aux_total, 8 * virtuals * aux_total),
        )(first_scalars, row_energy, col_energy, *left, *first)

    with jax.named_scope("last_pair"):
        high, low, dens_keep, dens_send = pl.pallas_call(
            last_pair_kernel,
            in_specs=[smem] * 2 + [vmem] * 13,
            out_specs=[vmem] * 4,
            out_shape=[
                shape(virtuals, aux_total, jnp.bfloat16),
                shape(virtuals, aux_total, jnp.bfloat16),
                shape(virtuals, half, jnp.float32),
                shape(virtuals, half, jnp.float32),
            ],
            scratch_shapes=[pltpu.VMEM((virtuals, virtuals), jnp.bfloat16)],
            compiler_params=params,
            cost_estimate=cost(square * (3 * aux_total + 2 * virtuals), 12 * virtuals * aux_total),
        )(
            place,
            last_scalars,
            row_energy,
            col_energy,
            *left,
            *last,
            grad,
            first_amp,
            first_mixed,
        )

    def gamma_block(step, high):
        metric_spec = pl.BlockSpec((1, width, aux_total), lambda i: (step, 0, 0))
        whole = pl.BlockSpec(grad_shape, lambda i: (0, 0))
        packed = pl.pallas_call(
            metric_kernel,
            grid=(1,),
            in_specs=[metric_spec, metric_spec, whole, whole],
            out_specs=pl.BlockSpec((width + TAIL_ROWS, virtuals), lambda i: (0, 0)),
            out_shape=shape(width + TAIL_ROWS, virtuals, jnp.bfloat16),
            compiler_params=params,
            cost_estimate=cost(
                6 * width * virtuals * aux_total, 4 * (width + virtuals) * aux_total
            ),
        )(metric_high, metric_low, high, low)
        return move(packed, lambda z, y, x, c: (z, c, x ^ (step >> 1), y ^ (step & 1)))

    layer_rows = virtuals // n_lay
    rows = virtuals // n_blk
    with jax.named_scope("gamma"):
        got_third = gamma_block(3, high)
    with jax.named_scope("density"):
        dens_got = core_swap(dens_send)
        coded = shape(layer_rows + TAIL_ROWS, half, jnp.bfloat16)
        layer, *messages = pl.pallas_call(
            density_layers_kernel,
            in_specs=[smem, vmem, vmem],
            out_specs=[vmem] * n_lay,
            out_shape=[shape(layer_rows, half, jnp.float32)] + [coded] * (n_lay - 1),
            compiler_params=params,
        )(place, dens_keep, dens_got)
        messages = [
            move(message, lambda z, y, x, c, step=step: (z ^ step, y, x, c))
            for step, message in enumerate(messages, 1)
        ]
    with jax.named_scope("gamma"):
        got_second = gamma_block(2, high)
        got_first = gamma_block(1, high)
        got_zeroth = gamma_block(0, high)
    with jax.named_scope("density"):
        mine, theirs = pl.pallas_call(
            density_rows_kernel,
            in_specs=[smem] + [vmem] * n_lay,
            out_specs=[vmem, vmem],
            out_shape=[shape(rows, half, jnp.float32)] * 2,
            scratch_shapes=[pltpu.VMEM((layer_rows, half), jnp.float32)],
            compiler_params=params,
        )(place, layer, *messages)
        from_x, from_y, from_xy = x_swap(mine), y_swap(theirs), xy_swap(theirs)
        block = (mine + from_x) + (from_y + from_xy)
        other = core_swap(block)
        density = jnp.where(
            c == 0,
            jnp.concatenate([block, other], 1),
            jnp.concatenate([other, block], 1),
        )
    with jax.named_scope("gamma"):
        gamma = pl.pallas_call(
            gamma_sum_kernel,
            in_specs=[vmem] * 4,
            out_specs=vmem,
            out_shape=jax.ShapeDtypeStruct((width, 1, virtuals), jnp.float32),
            compiler_params=params,
        )(got_third, got_second, got_first, got_zeroth)
    return gamma, density


def solution(mesh):
    n_blk, n_sec = mesh.shape["blk"], mesh.shape["sec"]

    def per_device(factors, occ_energy, vir_energy, metric):
        two_rows_of_layers = n_sec == 4 and n_blk == 2 * n_sec and factors.shape[0] == 1
        step = fast_device if two_rows_of_layers else general_device
        return step(factors, occ_energy, vir_energy, metric)

    return jax.shard_map(
        per_device,
        mesh=mesh,
        in_specs=(P("blk", None, "sec"), P(), P(), P()),
        out_specs=(P("sec", "blk", None), P("blk", None)),
        check_vma=False,
    )
```

```python
import functools

import jax
import jax.numpy as jnp
from jax import lax
from jax.experimental import pallas as pl
from jax.experimental.pallas import tpu as pltpu
from jax.sharding import PartitionSpec as P

CYCLE_STEPS = 4


def from_behind(shard, axis, by):
    devices = lax.axis_size(axis)
    return lax.ppermute(shard, axis, [(i, (i + by) % devices) for i in range(devices)])


def batch_energy(occ_energy, batch_index, per_batch):
    return lax.dynamic_slice_in_dim(occ_energy, batch_index * per_batch, per_batch, 0)


def pair_block(
    own_full, own_energy, partner, part_energy, vir_energy, acc_own, acc_part, density, weight
):
    per_batch = own_full.shape[0]

    def one_pair(pair_index, loop_state):
        acc_own, acc_part, density = loop_state
        first_pos = pair_index // per_batch
        second = pair_index % per_batch
        left_block = lax.dynamic_index_in_dim(own_full, first_pos, 0, keepdims=False)
        right_block = lax.dynamic_index_in_dim(partner, second, 0, keepdims=False)
        intersection = lax.dot_general(
            left_block, right_block, (((1,), (1,)), ((), ())), preferred_element_type=jnp.float32
        )
        energy_sum = lax.dynamic_index_in_dim(
            own_energy, first_pos, 0, keepdims=False
        ) + lax.dynamic_index_in_dim(part_energy, second, 0, keepdims=False)
        denominator = energy_sum - vir_energy[:, None] - vir_energy[None, :]
        amplitude = intersection / denominator
        mixed_amp = 2.0 * amplitude - amplitude.T
        amp_half = amplitude.astype(jnp.bfloat16)
        mixed_half = mixed_amp.astype(jnp.bfloat16)
        own_term = jnp.einsum(
            "bp,ab->pa", right_block, mixed_half, preferred_element_type=jnp.float32
        )
        acc_own = acc_own.at[first_pos].add(weight * own_term)
        dens_term = lax.dot_general(
            mixed_half, amp_half, (((1,), (1,)), ((), ())), preferred_element_type=jnp.float32
        )
        part_term = jnp.einsum(
            "ap,ab->pb", left_block, mixed_half, preferred_element_type=jnp.float32
        )
        acc_part = acc_part.at[second].add(weight * part_term)
        dens_term = dens_term + lax.dot_general(
            mixed_half, amp_half, (((0,), (0,)), ((), ())), preferred_element_type=jnp.float32
        )
        density = density + weight * dens_term
        return (acc_own, acc_part, density)

    return lax.fori_loop(0, per_batch * per_batch, one_pair, (acc_own, acc_part, density))


def general_device(factors, occ_energy, vir_energy, metric):
    n_blk = lax.axis_size("blk")
    n_sec = lax.axis_size("sec")
    blk_pos = lax.axis_index("blk")
    sec_pos = lax.axis_index("sec")
    per_batch = factors.shape[0]
    virtuals = factors.shape[1]
    aux_part = factors.shape[2]
    aux_total = aux_part * n_sec
    cycle_turns = min(CYCLE_STEPS, n_blk // (2 * n_sec))
    own_full = lax.all_gather(factors, "sec", axis=2, tiled=True)
    own_energy = batch_energy(occ_energy, blk_pos, per_batch)
    acc_own = jnp.zeros((per_batch, aux_total, virtuals), jnp.float32)
    density = jnp.zeros((virtuals, virtuals), jnp.float32)
    segmented = [factors]
    moving = factors
    for shift_turn in range(n_sec - 1):
        moving = from_behind(moving, "blk", 1)
        segmented.append(moving)
    partner = lax.all_to_all(
        jnp.stack(segmented, 0), "sec", split_axis=0, concat_axis=3, tiled=True
    )[0]
    acc_part = jnp.zeros((per_batch, aux_total, virtuals), jnp.float32)
    for cycle_step in range(cycle_turns):
        if cycle_step > 0:
            partner = from_behind(partner, "blk", n_sec)
            acc_part = from_behind(acc_part, "blk", n_sec)
        offset = sec_pos + n_sec * cycle_step
        weight = jnp.where(offset == 0, jnp.float32(0.5), jnp.float32(1.0))
        part_energy = batch_energy(occ_energy, (blk_pos - offset) % n_blk, per_batch)
        acc_own, acc_part, density = pair_block(
            own_full,
            own_energy,
            partner,
            part_energy,
            vir_energy,
            acc_own,
            acc_part,
            density,
            weight,
        )
    if cycle_turns > 1:
        acc_part = from_behind(acc_part, "blk", -n_sec * (cycle_turns - 1))
    regrouped = lax.all_to_all(acc_part[None], "sec", split_axis=2, concat_axis=0, tiled=True)
    carried = regrouped[n_sec - 1]
    for shift_turn in range(n_sec - 2, -1, -1):
        carried = from_behind(carried, "blk", -1) + regrouped[shift_turn]
    metric_rows = lax.dynamic_slice_in_dim(metric, sec_pos * aux_part, aux_part, 0)
    own_term = jnp.einsum("pq,ipa->qia", metric, acc_own, precision=lax.Precision.HIGHEST)
    gamma_part = lax.psum_scatter(
        own_term + jnp.einsum("pq,ipa->qia", metric_rows, carried, precision=lax.Precision.HIGHEST),
        "sec",
        scatter_dimension=0,
        tiled=True,
    )
    density_rows = lax.psum_scatter(density, "blk", scatter_dimension=0, tiled=True)
    density_out = lax.psum(density_rows, "sec")
    return (gamma_part, density_out)


AXES = ("blk", "sec")
NT = (((1,), (1,)), ((), ()))
NN = (((1,), (0,)), ((), ()))
TAIL_ROWS = 16
VMEM_LIMIT = 16 * 1024 * 1024


def dot(left, right, dims):
    return lax.dot_general(left, right, dims, preferred_element_type=jnp.float32)


def split_bits(device, n_sec):
    blk, sec = device // n_sec, device % n_sec
    return blk // 2, blk % 2, sec // 2, sec % 2


def join_bits(z, y, x, c, n_sec):
    return (2 * z + y) * n_sec + 2 * x + c


def send(value, target, n_blk, n_sec):
    pairs = []
    for device in range(n_blk * n_sec):
        pairs.append((device, join_bits(*target(*split_bits(device, n_sec)), n_sec)))
    return lax.ppermute(value, AXES, pairs)


def encode(value):
    peak = jnp.max(jnp.abs(value), keepdims=True)
    power = jnp.floor(15.4 - jnp.log2(jnp.maximum(peak, 1e-36)))
    power = jnp.clip(power, -120.0, 120.0)
    scaled = value * jnp.exp2(power)
    second = scaled * scaled
    fourth = second * second
    eighth = fourth * fourth
    coded = jnp.where(scaled < 0.0, -eighth, eighth).astype(jnp.bfloat16)
    tail = jnp.broadcast_to(power, (TAIL_ROWS, value.shape[1])).astype(jnp.bfloat16)
    return coded, tail


def encode_into(out, value):
    rows = value.shape[0]
    coded, tail = encode(value)
    out[:rows] = coded
    out[rows:] = tail


def decode(ref):
    rows = ref.shape[0] - TAIL_ROWS
    power = ref[rows:].astype(jnp.float32)[:1]
    coded = ref[:rows].astype(jnp.float32)
    root = jnp.exp2(jnp.log2(jnp.abs(coded)) * 0.125 - power)
    return jnp.where(coded < 0.0, -root, root)


def place_bits():
    blk, sec = lax.axis_index("blk"), lax.axis_index("sec")
    return blk // 2, blk % 2, sec // 2, sec % 2


def pair_terms(occupied, virtual, layer, left, right):
    z, y, x, c = place_bits()
    index = lax.broadcasted_iota(jnp.int32, occupied.shape, 1)

    def energy(batch):
        return jnp.sum(jnp.where(index == batch, occupied[...], 0.0), axis=1, keepdims=True)

    row_energy = virtual[...]
    row_sum = energy(2 * z + c) + energy(2 * layer + y) - row_energy
    size = row_energy.shape[1]
    col_energy = jnp.broadcast_to(row_energy, (128, size)).T[:, :1]
    col_sum = jnp.broadcast_to(row_sum, (128, size)).T[:, :1]
    straight = dot(left[0], right[0], NT)
    turned = dot(right[0], left[0], NT)
    for part in range(1, len(left)):
        straight += dot(left[part], right[part], NT)
        turned += dot(right[part], left[part], NT)
    amplitude = straight / (col_sum - row_energy)
    amplitude_t = turned / (row_sum - col_energy)
    return amplitude.astype(jnp.bfloat16), 2.0 * amplitude - amplitude_t


def read_left(refs):
    z, y, x, c = place_bits()
    home = c == y
    own, swapped, near, near_swapped, far, far_swapped = [ref[...] for ref in refs]
    return [
        jnp.where(home, own, near),
        jnp.where(home, swapped, near_swapped),
        jnp.where(home, near, far),
        jnp.where(home, near_swapped, far_swapped),
    ]


def first_pair_kernel(*refs):
    z, y, x, c = place_bits()
    left = read_left(refs[2:8])
    right = [ref[...] for ref in refs[8:12]]
    grad_out, amp_out, mixed_out = refs[-3:]
    layer = jnp.where(x == 1, z, z ^ 1)
    amp_half, mixed = pair_terms(refs[0], refs[1], layer, left, right)
    mixed_half = mixed.astype(jnp.bfloat16)
    width = right[0].shape[1]
    for part in range(4):
        grad_out[:, part * width : (part + 1) * width] = dot(mixed_half, right[part], NN)
    amp_out[...] = amp_half
    mixed_out[...] = mixed_half


def last_pair_kernel(*refs):
    z, y, x, c = place_bits()
    left = read_left(refs[2:8])
    right = [ref[...] for ref in refs[8:12]]
    first_amp, first_mixed = refs[12:14]
    mixed_out, dens_keep, dens_send, amp = refs[-4:]
    layer = jnp.where(x == 1, z ^ 3, z ^ 2)
    amp_half, mixed = pair_terms(refs[0], refs[1], layer, left, right)
    outside = (x == 0) & (c == y)
    mixed_half = jnp.where(outside, 0.0, mixed).astype(jnp.bfloat16)
    amp[...] = amp_half
    mixed_out[...] = mixed_half
    half = amp.shape[0] // 2
    mixed_first = first_mixed[...]
    for out, core in ((dens_send, 1 - c), (dens_keep, c)):
        rows = pl.ds(pl.multiple_of(core * half, half), half)
        out[...] = dot(mixed_half, amp[rows, :], NT) + dot(mixed_first, first_amp[rows, :], NT)


def metric_product(step, metric_high, metric_low, high, low):
    metric_top = metric_high[step]
    block = dot(metric_top, high[...], NT)
    block += dot(metric_top, low[...], NT)
    return block + dot(metric_low[step], high[...], NT)


def gradient_kernel(step, mixed, *refs):
    grad_in, metric_high, metric_low, high_out, low_out, out = refs[4:]
    mixed_half = mixed[...]
    width = refs[0].shape[1]
    for part in range(4):
        cols = slice(part * width, (part + 1) * width)
        grad = grad_in[:, cols] + dot(mixed_half, refs[part][...], NN)
        high = grad.astype(jnp.bfloat16)
        high_out[:, cols] = high
        low_out[:, cols] = (grad - high.astype(jnp.float32)).astype(jnp.bfloat16)
    encode_into(out, metric_product(step, metric_high, metric_low, high_out, low_out))


def metric_kernel(step, metric_high, metric_low, high, low, *refs):
    encode_into(refs[-1], metric_product(step, metric_high, metric_low, high, low))


def turn_metric_kernel(metric, *refs):
    high, low = refs[-2:]
    z, y, x, c = place_bits()
    steps, width, aux_total = high.shape
    row = lax.broadcasted_iota(jnp.int32, (width, width), 0)
    col = lax.broadcasted_iota(jnp.int32, (width, width), 1)
    unit = jnp.where(row == col, 1.0, 0.0).astype(jnp.bfloat16)
    lane = 2 * x + c
    for step in range(steps):
        target = 2 * (x ^ (step >> 1)) + (y ^ (step & 1))
        for part, order in enumerate((lane, lane ^ 2, lane ^ 1, lane ^ 3)):
            value = metric[
                pl.ds(pl.multiple_of(order * width, width), width),
                pl.ds(pl.multiple_of(target * width, width), width),
            ]
            top = value.astype(jnp.bfloat16)
            rest = (value - top.astype(jnp.float32)).astype(jnp.bfloat16)
            cols = slice(part * width, (part + 1) * width)
            high[step, :, cols] = dot(unit, top, NT).astype(jnp.bfloat16)
            low[step, :, cols] = dot(unit, rest, NT).astype(jnp.bfloat16)


def gamma_part_kernel(left, right, *refs):
    refs[-1][...] = decode(left) + decode(right)


def gamma_sum_kernel(part, left, right, *refs):
    refs[-1][:, 0, :] = part[...] + decode(left) + decode(right)


def halve(total, bit, keep_out, send_out):
    rows = keep_out.shape[0]
    keep_out[...] = total[pl.ds(pl.multiple_of(bit * rows, rows), rows), :]
    encode_into(send_out, total[pl.ds(pl.multiple_of((1 - bit) * rows, rows), rows), :])


def density_cores_kernel(keep, got, *refs):
    keep_out, send_out, total = refs[-3:]
    z, y, x, c = place_bits()
    total[...] = keep[...] + got[...]
    halve(total, z // 2, keep_out, send_out)


def density_layers_kernel(keep, got, *refs):
    keep_out, send_out, total = refs[-3:]
    z, y, x, c = place_bits()
    total[...] = keep[...] + decode(got)
    halve(total, z % 2, keep_out, send_out)


def density_rows_kernel(keep, got, *refs):
    mine, theirs, total = refs[-3:]
    z, y, x, c = place_bits()
    total[...] = keep[...] + decode(got)
    rows = mine.shape[0]
    mine[...] = total[pl.ds(pl.multiple_of(y * rows, rows), rows), :]
    theirs[...] = total[pl.ds(pl.multiple_of((1 - y) * rows, rows), rows), :]


def density_block_kernel(mine, from_x, from_y, from_xy, *refs):
    refs[-1][...] = (mine[...] + from_x[...]) + (from_y[...] + from_xy[...])


def density_join_kernel(block, other, out):
    z, y, x, c = place_bits()
    half = block.shape[1]
    out[:, :half] = jnp.where(c == 0, block[...], other[...])
    out[:, half:] = jnp.where(c == 0, other[...], block[...])


def fast_device(factors, occ_energy, vir_energy, metric):
    n_blk = lax.axis_size("blk")
    n_sec = lax.axis_size("sec")
    own = factors[0]
    virtuals, width = own.shape
    aux_total = width * n_sec
    half = virtuals // 2
    rows = virtuals // n_blk
    square = 2 * virtuals * virtuals

    def move(value, target):
        return send(value, target, n_blk, n_sec)

    def core_swap(value):
        return move(value, lambda z, y, x, c: (z, y, x, 1 - c))

    def x_swap(value):
        return move(value, lambda z, y, x, c: (z, y, 1 - x, c))

    def y_swap(value):
        return move(value, lambda z, y, x, c: (z, 1 - y, x, c))

    def xy_swap(value):
        return move(value, lambda z, y, x, c: (z, 1 - y, 1 - x, c))

    def first_partner(value):
        return move(value, lambda z, y, x, c: (z if x else z ^ 1, y, x, c))

    def last_partner(value):
        return move(value, lambda z, y, x, c: (z ^ 3 if x else z ^ 2, y, x, c))

    def near_left(value):
        return move(value, lambda z, y, x, c: (z, 1 - y, x, c) if c == y else (z, y, x, 1 - c))

    def far_left(value):
        return move(value, lambda z, y, x, c: (z, y, x, c) if c == y else (z, 1 - y, x, 1 - c))

    vmem = pl.BlockSpec(memory_space=pltpu.VMEM)
    unread = pl.BlockSpec(memory_space=pl.ANY)
    params = pltpu.CompilerParams(vmem_limit_bytes=VMEM_LIMIT)

    def shape(dtype, *dims):
        return jax.ShapeDtypeStruct(dims, dtype)

    def call(name, kernel, outs, operands, earlier=(), scratch=(), flops=0):
        many = isinstance(outs, list)
        with jax.named_scope(name):
            return pl.pallas_call(
                kernel,
                in_specs=[vmem] * len(operands) + [unread] * len(earlier),
                out_specs=[vmem] * len(outs) if many else vmem,
                out_shape=outs,
                scratch_shapes=list(scratch),
                compiler_params=params,
                cost_estimate=pl.CostEstimate(
                    flops=flops,
                    bytes_accessed=sum(2 * operand.size for operand in operands),
                    transcendentals=0,
                ),
            )(*operands, *earlier)

    with jax.named_scope("gather"):
        far_own, near_own, swapped, first_own, last_own = lax.optimization_barrier(
            (far_left(own), near_left(own), x_swap(own), first_partner(own), last_partner(own))
        )

    metric_high, metric_low = call(
        "metric_turn",
        turn_metric_kernel,
        [shape(jnp.bfloat16, n_sec, width, aux_total)] * 2,
        [metric],
        [swapped],
        flops=4 * aux_total * aux_total * width,
    )

    with jax.named_scope("gather"):
        (
            far_swapped,
            near_swapped,
            first_swapped,
            last_swapped,
            last_own_got,
            first_own_got,
            metric_high,
            metric_low,
        ) = lax.optimization_barrier(
            (
                far_left(swapped),
                near_left(swapped),
                first_partner(swapped),
                last_partner(swapped),
                core_swap(last_own),
                core_swap(first_own),
                metric_high,
                metric_low,
            )
        )
        left = [own, swapped, near_own, near_swapped, far_own, far_swapped]
        first = [first_own, first_swapped, first_own_got, core_swap(first_swapped)]
        last = [last_own, last_swapped, last_own_got, core_swap(last_swapped)]

    energies = [occ_energy[None, :], vir_energy[None, :]]
    pair_flops = 3 * square * aux_total
    grad, first_amp, first_mixed = call(
        "first_pair",
        first_pair_kernel,
        [
            shape(jnp.float32, virtuals, aux_total),
            shape(jnp.bfloat16, virtuals, virtuals),
            shape(jnp.bfloat16, virtuals, virtuals),
        ],
        energies + left + first,
        flops=pair_flops,
    )
    last_mixed, dens_keep, dens_send = call(
        "last_pair",
        last_pair_kernel,
        [
            shape(jnp.bfloat16, virtuals, virtuals),
            shape(jnp.float32, virtuals, half),
            shape(jnp.float32, virtuals, half),
        ],
        energies + left + last + [first_amp, first_mixed],
        scratch=[pltpu.VMEM((virtuals, virtuals), jnp.bfloat16)],
        flops=pair_flops,
    )
    dens_got = core_swap(dens_send)

    message = shape(jnp.bfloat16, width + TAIL_ROWS, virtuals)
    block_flops = 6 * width * virtuals * aux_total
    high, low, third = call(
        "gradient",
        functools.partial(gradient_kernel, 3),
        [
            shape(jnp.bfloat16, virtuals, aux_total),
            shape(jnp.bfloat16, virtuals, aux_total),
            message,
        ],
        [last_mixed, *last, grad, metric_high, metric_low],
        flops=2 * block_flops,
    )

    def gamma_block(step, *earlier):
        return call(
            "gamma_block",
            functools.partial(metric_kernel, step),
            message,
            [metric_high, metric_low, high, low],
            earlier,
            flops=block_flops,
        )

    def gamma_move(step, block):
        return move(block, lambda z, y, x, c: (z, c, x ^ (step >> 1), y ^ (step & 1)))

    def density_half(name, kernel, count, keep, got, *earlier):
        return call(
            name,
            kernel,
            [
                shape(jnp.float32, count, half),
                shape(jnp.bfloat16, count + TAIL_ROWS, half),
            ],
            [keep, got],
            earlier,
            [pltpu.VMEM(keep.shape, jnp.float32)],
        )

    got_third = gamma_move(3, third)
    keep, packed = density_half(
        "density_cores", density_cores_kernel, 4 * rows, dens_keep, dens_got, third
    )
    got = move(packed, lambda z, y, x, c: (z ^ 2, y, x, c))
    second = gamma_block(2, packed)
    got_second = gamma_move(2, second)
    first_block = gamma_block(1, second)
    got_first = gamma_move(1, first_block)
    keep, packed = density_half(
        "density_layers", density_layers_kernel, 2 * rows, keep, got, first_block, got_third
    )
    got = move(packed, lambda z, y, x, c: (z ^ 1, y, x, c))
    zeroth = gamma_block(0, packed)
    got_zeroth = gamma_move(0, zeroth)
    mine, theirs = call(
        "density_rows",
        density_rows_kernel,
        [shape(jnp.float32, rows, half)] * 2,
        [keep, got],
        [zeroth, got_second],
        [pltpu.VMEM(keep.shape, jnp.float32)],
    )
    from_x, from_y, from_xy = x_swap(mine), y_swap(theirs), xy_swap(theirs)
    part = call(
        "gamma_part",
        gamma_part_kernel,
        shape(jnp.float32, width, virtuals),
        [got_third, got_second],
        [mine],
    )
    block = call(
        "density_block",
        density_block_kernel,
        shape(jnp.float32, rows, half),
        [mine, from_x, from_y, from_xy],
        [part, got_first],
    )
    other = core_swap(block)
    gamma = call(
        "gamma_sum",
        gamma_sum_kernel,
        shape(jnp.float32, width, 1, virtuals),
        [part, got_first, got_zeroth],
        [block],
    )
    density = call(
        "density_join",
        density_join_kernel,
        shape(jnp.float32, rows, virtuals),
        [block, other],
    )
    return gamma, density


def solution(mesh):
    n_blk, n_sec = mesh.shape["blk"], mesh.shape["sec"]

    def per_device(factors, occ_energy, vir_energy, metric):
        two_rows_of_layers = n_sec == 4 and n_blk == 2 * n_sec and factors.shape[0] == 1
        step = fast_device if two_rows_of_layers else general_device
        return step(factors, occ_energy, vir_energy, metric)

    return jax.shard_map(
        per_device,
        mesh=mesh,
        in_specs=(P("blk", None, "sec"), P(), P(), P()),
        out_specs=(P("sec", "blk", None), P("blk", None)),
        check_vma=False,
    )
```

```python
import functools

import jax
import jax.numpy as jnp
from jax import lax
from jax.experimental import pallas as pl
from jax.experimental.pallas import tpu as pltpu
from jax.sharding import PartitionSpec as P

CYCLE_STEPS = 4


def from_behind(shard, axis, by):
    devices = lax.axis_size(axis)
    return lax.ppermute(shard, axis, [(i, (i + by) % devices) for i in range(devices)])


def batch_energy(occ_energy, batch_index, per_batch):
    return lax.dynamic_slice_in_dim(occ_energy, batch_index * per_batch, per_batch, 0)


def pair_block(
    own_full, own_energy, partner, part_energy, vir_energy, acc_own, acc_part, density, weight
):
    per_batch = own_full.shape[0]

    def one_pair(pair_index, loop_state):
        acc_own, acc_part, density = loop_state
        first_pos = pair_index // per_batch
        second = pair_index % per_batch
        left_block = lax.dynamic_index_in_dim(own_full, first_pos, 0, keepdims=False)
        right_block = lax.dynamic_index_in_dim(partner, second, 0, keepdims=False)
        intersection = lax.dot_general(
            left_block, right_block, (((1,), (1,)), ((), ())), preferred_element_type=jnp.float32
        )
        energy_sum = lax.dynamic_index_in_dim(
            own_energy, first_pos, 0, keepdims=False
        ) + lax.dynamic_index_in_dim(part_energy, second, 0, keepdims=False)
        denominator = energy_sum - vir_energy[:, None] - vir_energy[None, :]
        amplitude = intersection / denominator
        mixed_amp = 2.0 * amplitude - amplitude.T
        amp_half = amplitude.astype(jnp.bfloat16)
        mixed_half = mixed_amp.astype(jnp.bfloat16)
        own_term = jnp.einsum(
            "bp,ab->pa", right_block, mixed_half, preferred_element_type=jnp.float32
        )
        acc_own = acc_own.at[first_pos].add(weight * own_term)
        dens_term = lax.dot_general(
            mixed_half, amp_half, (((1,), (1,)), ((), ())), preferred_element_type=jnp.float32
        )
        part_term = jnp.einsum(
            "ap,ab->pb", left_block, mixed_half, preferred_element_type=jnp.float32
        )
        acc_part = acc_part.at[second].add(weight * part_term)
        dens_term = dens_term + lax.dot_general(
            mixed_half, amp_half, (((0,), (0,)), ((), ())), preferred_element_type=jnp.float32
        )
        density = density + weight * dens_term
        return (acc_own, acc_part, density)

    return lax.fori_loop(0, per_batch * per_batch, one_pair, (acc_own, acc_part, density))


def general_device(factors, occ_energy, vir_energy, metric):
    n_blk = lax.axis_size("blk")
    n_sec = lax.axis_size("sec")
    blk_pos = lax.axis_index("blk")
    sec_pos = lax.axis_index("sec")
    per_batch = factors.shape[0]
    virtuals = factors.shape[1]
    aux_part = factors.shape[2]
    aux_total = aux_part * n_sec
    cycle_turns = min(CYCLE_STEPS, n_blk // (2 * n_sec))
    own_full = lax.all_gather(factors, "sec", axis=2, tiled=True)
    own_energy = batch_energy(occ_energy, blk_pos, per_batch)
    acc_own = jnp.zeros((per_batch, aux_total, virtuals), jnp.float32)
    density = jnp.zeros((virtuals, virtuals), jnp.float32)
    segmented = [factors]
    moving = factors
    for shift_turn in range(n_sec - 1):
        moving = from_behind(moving, "blk", 1)
        segmented.append(moving)
    partner = lax.all_to_all(
        jnp.stack(segmented, 0), "sec", split_axis=0, concat_axis=3, tiled=True
    )[0]
    acc_part = jnp.zeros((per_batch, aux_total, virtuals), jnp.float32)
    for cycle_step in range(cycle_turns):
        if cycle_step > 0:
            partner = from_behind(partner, "blk", n_sec)
            acc_part = from_behind(acc_part, "blk", n_sec)
        offset = sec_pos + n_sec * cycle_step
        weight = jnp.where(offset == 0, jnp.float32(0.5), jnp.float32(1.0))
        part_energy = batch_energy(occ_energy, (blk_pos - offset) % n_blk, per_batch)
        acc_own, acc_part, density = pair_block(
            own_full,
            own_energy,
            partner,
            part_energy,
            vir_energy,
            acc_own,
            acc_part,
            density,
            weight,
        )
    if cycle_turns > 1:
        acc_part = from_behind(acc_part, "blk", -n_sec * (cycle_turns - 1))
    regrouped = lax.all_to_all(acc_part[None], "sec", split_axis=2, concat_axis=0, tiled=True)
    carried = regrouped[n_sec - 1]
    for shift_turn in range(n_sec - 2, -1, -1):
        carried = from_behind(carried, "blk", -1) + regrouped[shift_turn]
    metric_rows = lax.dynamic_slice_in_dim(metric, sec_pos * aux_part, aux_part, 0)
    own_term = jnp.einsum("pq,ipa->qia", metric, acc_own, precision=lax.Precision.HIGHEST)
    gamma_part = lax.psum_scatter(
        own_term + jnp.einsum("pq,ipa->qia", metric_rows, carried, precision=lax.Precision.HIGHEST),
        "sec",
        scatter_dimension=0,
        tiled=True,
    )
    density_rows = lax.psum_scatter(density, "blk", scatter_dimension=0, tiled=True)
    density_out = lax.psum(density_rows, "sec")
    return (gamma_part, density_out)


AXES = ("blk", "sec")
NT = (((1,), (1,)), ((), ()))
NN = (((1,), (0,)), ((), ()))
TAIL_ROWS = 16
VMEM_LIMIT = 16 * 1024 * 1024


def dot(left, right, dims):
    return lax.dot_general(left, right, dims, preferred_element_type=jnp.float32)


def split_bits(device, n_sec):
    blk, sec = device // n_sec, device % n_sec
    return blk // 2, blk % 2, sec // 2, sec % 2


def join_bits(z, y, x, c, n_sec):
    return (2 * z + y) * n_sec + 2 * x + c


def send(value, target, n_blk, n_sec):
    pairs = []
    for device in range(n_blk * n_sec):
        pairs.append((device, join_bits(*target(*split_bits(device, n_sec)), n_sec)))
    return lax.ppermute(value, AXES, pairs)


def encode(value):
    peak = jnp.max(jnp.abs(value), keepdims=True)
    power = jnp.floor(15.4 - jnp.log2(jnp.maximum(peak, 1e-36)))
    power = jnp.clip(power, -120.0, 120.0)
    scaled = value * jnp.exp2(power)
    second = scaled * scaled
    fourth = second * second
    eighth = fourth * fourth
    coded = jnp.where(scaled < 0.0, -eighth, eighth).astype(jnp.bfloat16)
    tail = jnp.broadcast_to(power, (TAIL_ROWS, value.shape[1])).astype(jnp.bfloat16)
    return coded, tail


def encode_into(out, value):
    rows = value.shape[0]
    coded, tail = encode(value)
    out[:rows] = coded
    out[rows:] = tail


def decode(ref):
    rows = ref.shape[0] - TAIL_ROWS
    power = ref[rows:].astype(jnp.float32)[:1]
    coded = ref[:rows].astype(jnp.float32)
    root = jnp.exp2(jnp.log2(jnp.abs(coded)) * 0.125 - power)
    return jnp.where(coded < 0.0, -root, root)


def place_bits():
    blk, sec = lax.axis_index("blk"), lax.axis_index("sec")
    return blk // 2, blk % 2, sec // 2, sec % 2


def pair_terms(occupied, virtual, layer, left, right):
    z, y, x, c = place_bits()
    index = lax.broadcasted_iota(jnp.int32, occupied.shape, 1)

    def energy(batch):
        return jnp.sum(jnp.where(index == batch, occupied[...], 0.0), axis=1, keepdims=True)

    row_energy = virtual[...]
    row_sum = energy(2 * z + c) + energy(2 * layer + y) - row_energy
    size = row_energy.shape[1]
    col_energy = jnp.broadcast_to(row_energy, (128, size)).T[:, :1]
    col_sum = jnp.broadcast_to(row_sum, (128, size)).T[:, :1]
    straight = dot(left[0], right[0], NT)
    turned = dot(right[0], left[0], NT)
    for part in range(1, len(left)):
        straight += dot(left[part], right[part], NT)
        turned += dot(right[part], left[part], NT)
    amplitude = straight / (col_sum - row_energy)
    amplitude_t = turned / (row_sum - col_energy)
    return amplitude.astype(jnp.bfloat16), 2.0 * amplitude - amplitude_t


def read_left(refs):
    z, y, x, c = place_bits()
    home = c == y
    own, swapped, near, near_swapped, far, far_swapped = [ref[...] for ref in refs]
    return [
        jnp.where(home, own, near),
        jnp.where(home, swapped, near_swapped),
        jnp.where(home, near, far),
        jnp.where(home, near_swapped, far_swapped),
    ]


def first_pair_kernel(*refs):
    z, y, x, c = place_bits()
    left = read_left(refs[2:8])
    right = [ref[...] for ref in refs[8:12]]
    grad_out, amp_out, mixed_out = refs[-3:]
    layer = jnp.where(x == 1, z, z ^ 1)
    amp_half, mixed = pair_terms(refs[0], refs[1], layer, left, right)
    mixed_half = mixed.astype(jnp.bfloat16)
    width = right[0].shape[1]
    for part in range(4):
        grad_out[:, part * width : (part + 1) * width] = dot(mixed_half, right[part], NN)
    amp_out[...] = amp_half
    mixed_out[...] = mixed_half


def last_pair_kernel(*refs):
    z, y, x, c = place_bits()
    left = read_left(refs[2:8])
    right = [ref[...] for ref in refs[8:12]]
    amp_out, mixed_out = refs[-2:]
    layer = jnp.where(x == 1, z ^ 3, z ^ 2)
    amp_half, mixed = pair_terms(refs[0], refs[1], layer, left, right)
    outside = (x == 0) & (c == y)
    amp_out[...] = amp_half
    mixed_out[...] = jnp.where(outside, 0.0, mixed).astype(jnp.bfloat16)


def density_pairs_kernel(first_amp, first_mixed, last_amp, last_mixed, keep_out, send_out):
    z, y, x, c = place_bits()
    half = keep_out.shape[1]
    for out, core in ((send_out, 1 - c), (keep_out, c)):
        rows = pl.ds(pl.multiple_of(core * half, half), half)
        first = dot(first_mixed[...], first_amp[rows, :], NT)
        out[...] = first + dot(last_mixed[...], last_amp[rows, :], NT)


def metric_product(step, metric_high, metric_low, high, low):
    metric_top = metric_high[step]
    block = dot(metric_top, high[...], NT)
    block += dot(metric_top, low[...], NT)
    return block + dot(metric_low[step], high[...], NT)


def gradient_kernel(step, mixed, *refs):
    grad_in, metric_high, metric_low, high_out, low_out, out = refs[4:]
    mixed_half = mixed[...]
    width = refs[0].shape[1]
    for part in range(4):
        cols = slice(part * width, (part + 1) * width)
        grad = grad_in[:, cols] + dot(mixed_half, refs[part][...], NN)
        high = grad.astype(jnp.bfloat16)
        high_out[:, cols] = high
        low_out[:, cols] = (grad - high.astype(jnp.float32)).astype(jnp.bfloat16)
    encode_into(out, metric_product(step, metric_high, metric_low, high_out, low_out))


def metric_kernel(step, metric_high, metric_low, high, low, *refs):
    encode_into(refs[-1], metric_product(step, metric_high, metric_low, high, low))


def turn_metric_kernel(metric, *refs):
    high, low = refs[-2:]
    z, y, x, c = place_bits()
    steps, width, aux_total = high.shape
    row = lax.broadcasted_iota(jnp.int32, (width, width), 0)
    col = lax.broadcasted_iota(jnp.int32, (width, width), 1)
    unit = jnp.where(row == col, 1.0, 0.0).astype(jnp.bfloat16)
    lane = 2 * x + c
    for step in range(steps):
        target = 2 * (x ^ (step >> 1)) + (y ^ (step & 1))
        for part, order in enumerate((lane, lane ^ 2, lane ^ 1, lane ^ 3)):
            value = metric[
                pl.ds(pl.multiple_of(order * width, width), width),
                pl.ds(pl.multiple_of(target * width, width), width),
            ]
            top = value.astype(jnp.bfloat16)
            rest = (value - top.astype(jnp.float32)).astype(jnp.bfloat16)
            cols = slice(part * width, (part + 1) * width)
            high[step, :, cols] = dot(unit, top, NT).astype(jnp.bfloat16)
            low[step, :, cols] = dot(unit, rest, NT).astype(jnp.bfloat16)


def gamma_part_kernel(left, right, *refs):
    refs[-1][...] = decode(left) + decode(right)


def gamma_sum_kernel(part, left, right, *refs):
    refs[-1][:, 0, :] = part[...] + decode(left) + decode(right)


def halve(total, bit, keep_out, send_out):
    rows = keep_out.shape[0]
    keep_out[...] = total[pl.ds(pl.multiple_of(bit * rows, rows), rows), :]
    encode_into(send_out, total[pl.ds(pl.multiple_of((1 - bit) * rows, rows), rows), :])


def density_cores_kernel(keep, got, *refs):
    keep_out, send_out, total = refs[-3:]
    z, y, x, c = place_bits()
    total[...] = keep[...] + got[...]
    halve(total, z // 2, keep_out, send_out)


def density_layers_kernel(keep, got, *refs):
    keep_out, send_out, total = refs[-3:]
    z, y, x, c = place_bits()
    total[...] = keep[...] + decode(got)
    halve(total, z % 2, keep_out, send_out)


def density_rows_kernel(keep, got, *refs):
    mine, theirs, total = refs[-3:]
    z, y, x, c = place_bits()
    total[...] = keep[...] + decode(got)
    rows = mine.shape[0]
    mine[...] = total[pl.ds(pl.multiple_of(y * rows, rows), rows), :]
    theirs[...] = total[pl.ds(pl.multiple_of((1 - y) * rows, rows), rows), :]


def density_block_kernel(mine, from_x, from_y, from_xy, *refs):
    refs[-1][...] = (mine[...] + from_x[...]) + (from_y[...] + from_xy[...])


def density_join_kernel(block, other, out):
    z, y, x, c = place_bits()
    half = block.shape[1]
    out[:, :half] = jnp.where(c == 0, block[...], other[...])
    out[:, half:] = jnp.where(c == 0, other[...], block[...])


def fast_device(factors, occ_energy, vir_energy, metric):
    n_blk = lax.axis_size("blk")
    n_sec = lax.axis_size("sec")
    own = factors[0]
    virtuals, width = own.shape
    aux_total = width * n_sec
    half = virtuals // 2
    rows = virtuals // n_blk
    square = 2 * virtuals * virtuals

    def move(value, target):
        return send(value, target, n_blk, n_sec)

    def core_swap(value):
        return move(value, lambda z, y, x, c: (z, y, x, 1 - c))

    def x_swap(value):
        return move(value, lambda z, y, x, c: (z, y, 1 - x, c))

    def y_swap(value):
        return move(value, lambda z, y, x, c: (z, 1 - y, x, c))

    def xy_swap(value):
        return move(value, lambda z, y, x, c: (z, 1 - y, 1 - x, c))

    def first_partner(value):
        return move(value, lambda z, y, x, c: (z if x else z ^ 1, y, x, c))

    def first_partner_cross(value):
        return move(value, lambda z, y, x, c: (z ^ 1 if x else z, y, 1 - x, c))

    def last_partner(value):
        return move(value, lambda z, y, x, c: (z ^ 3 if x else z ^ 2, y, x, c))

    def last_partner_cross(value):
        return move(value, lambda z, y, x, c: (z ^ 2 if x else z ^ 3, y, 1 - x, c))

    def near_left(value):
        return move(value, lambda z, y, x, c: (z, 1 - y, x, c) if c == y else (z, y, x, 1 - c))

    def far_left(value):
        return move(value, lambda z, y, x, c: (z, y, x, c) if c == y else (z, 1 - y, x, 1 - c))

    vmem = pl.BlockSpec(memory_space=pltpu.VMEM)
    unread = pl.BlockSpec(memory_space=pl.ANY)
    params = pltpu.CompilerParams(vmem_limit_bytes=VMEM_LIMIT)

    def shape(dtype, *dims):
        return jax.ShapeDtypeStruct(dims, dtype)

    def call(name, kernel, outs, operands, earlier=(), scratch=(), flops=0):
        many = isinstance(outs, list)
        with jax.named_scope(name):
            return pl.pallas_call(
                kernel,
                in_specs=[vmem] * len(operands) + [unread] * len(earlier),
                out_specs=[vmem] * len(outs) if many else vmem,
                out_shape=outs,
                scratch_shapes=list(scratch),
                compiler_params=params,
                cost_estimate=pl.CostEstimate(
                    flops=flops,
                    bytes_accessed=0,
                    transcendentals=0,
                ),
            )(*operands, *earlier)

    metric_high, metric_low = call(
        "metric_turn",
        turn_metric_kernel,
        [shape(jnp.bfloat16, n_sec, width, aux_total)] * 2,
        [metric],
        flops=4 * aux_total * aux_total * width,
    )
    with jax.named_scope("gather"):
        swapped, last_own, metric_high, metric_low = (
            lax.optimization_barrier(
                (
                    x_swap(own),
                    last_partner(own),
                    metric_high,
                    metric_low,
                )
            )
        )
        far_own, near_own, first_own, first_cross, last_swapped = lax.optimization_barrier(
            (
                far_left(own),
                near_left(own),
                first_partner(own),
                first_partner_cross(own),
                last_partner(swapped),
            )
        )
        far_swapped, near_swapped = far_left(swapped), near_left(swapped)
        left = [own, swapped, near_own, near_swapped, far_own, far_swapped]
        first = [first_own, first_cross, core_swap(first_own), core_swap(first_cross)]
        last = [last_own, last_swapped, core_swap(last_own), core_swap(last_swapped)]

    energies = [occ_energy[None, :], vir_energy[None, :]]
    half_square = shape(jnp.bfloat16, virtuals, virtuals)
    grad, first_amp, first_mixed = call(
        "first_pair",
        first_pair_kernel,
        [shape(jnp.float32, virtuals, aux_total), half_square, half_square],
        energies + left + first,
    )
    last_amp, last_mixed = call(
        "last_pair",
        last_pair_kernel,
        [half_square, half_square],
        energies + left + last,
        [first_amp],
        flops=4 * square * aux_total,
    )
    dens_keep, dens_send = call(
        "density_pairs",
        density_pairs_kernel,
        [shape(jnp.float32, virtuals, half)] * 2,
        [first_amp, first_mixed, last_amp, last_mixed],
        flops=2 * square * virtuals,
    )
    dens_got = core_swap(dens_send)

    message = shape(jnp.bfloat16, width + TAIL_ROWS, virtuals)
    block_flops = 6 * width * virtuals * aux_total
    high, low, third = call(
        "gradient",
        functools.partial(gradient_kernel, 3),
        [
            shape(jnp.bfloat16, virtuals, aux_total),
            shape(jnp.bfloat16, virtuals, aux_total),
            message,
        ],
        [last_mixed, *last, grad, metric_high, metric_low],
        flops=2 * block_flops,
    )

    def gamma_block(step, *earlier):
        return call(
            "gamma_block",
            functools.partial(metric_kernel, step),
            message,
            [metric_high, metric_low, high, low],
            earlier,
            flops=block_flops,
        )

    def gamma_move(step, block):
        return move(block, lambda z, y, x, c: (z, c, x ^ (step >> 1), y ^ (step & 1)))

    def density_half(name, kernel, count, keep, got, *earlier):
        return call(
            name,
            kernel,
            [
                shape(jnp.float32, count, half),
                shape(jnp.bfloat16, count + TAIL_ROWS, half),
            ],
            [keep, got],
            earlier,
            [pltpu.VMEM(keep.shape, jnp.float32)],
        )

    got_third = gamma_move(3, third)
    keep, packed = density_half(
        "density_cores", density_cores_kernel, 4 * rows, dens_keep, dens_got, third
    )
    got = move(packed, lambda z, y, x, c: (z ^ 2, y, x, c))
    second = gamma_block(2, packed)
    got_second = gamma_move(2, second)
    first_block = gamma_block(1, second)
    got_first = gamma_move(1, first_block)
    zeroth = gamma_block(0, first_block)
    got_zeroth = gamma_move(0, zeroth)
    keep, packed = density_half(
        "density_layers", density_layers_kernel, 2 * rows, keep, got, zeroth
    )
    got = move(packed, lambda z, y, x, c: (z ^ 1, y, x, c))
    mine, theirs = call(
        "density_rows",
        density_rows_kernel,
        [shape(jnp.float32, rows, half)] * 2,
        [keep, got],
        [got_third],
        [pltpu.VMEM(keep.shape, jnp.float32)],
    )
    from_x, from_y, from_xy = x_swap(mine), y_swap(theirs), xy_swap(theirs)
    part = call(
        "gamma_part",
        gamma_part_kernel,
        shape(jnp.float32, width, virtuals),
        [got_third, got_second],
        [mine],
    )
    block = call(
        "density_block",
        density_block_kernel,
        shape(jnp.float32, rows, half),
        [mine, from_x, from_y, from_xy],
        [part, got_first],
    )
    other = core_swap(block)
    gamma = call(
        "gamma_sum",
        gamma_sum_kernel,
        shape(jnp.float32, width, 1, virtuals),
        [part, got_first, got_zeroth],
        [block],
    )
    density = call(
        "density_join",
        density_join_kernel,
        shape(jnp.float32, rows, virtuals),
        [block, other],
    )
    return gamma, density


def solution(mesh):
    n_blk, n_sec = mesh.shape["blk"], mesh.shape["sec"]

    def per_device(factors, occ_energy, vir_energy, metric):
        two_rows_of_layers = n_sec == 4 and n_blk == 2 * n_sec and factors.shape[0] == 1
        step = fast_device if two_rows_of_layers else general_device
        return step(factors, occ_energy, vir_energy, metric)

    return jax.shard_map(
        per_device,
        mesh=mesh,
        in_specs=(P("blk", None, "sec"), P(), P(), P()),
        out_specs=(P("sec", "blk", None), P("blk", None)),
        check_vma=False,
    )
```

```python
import functools

import jax
import jax.numpy as jnp
from jax import lax
from jax.experimental import pallas as pl
from jax.experimental.pallas import tpu as pltpu
from jax.sharding import PartitionSpec as P

CYCLE_STEPS = 4


def from_behind(shard, axis, by):
    devices = lax.axis_size(axis)
    return lax.ppermute(shard, axis, [(i, (i + by) % devices) for i in range(devices)])


def batch_energy(occ_energy, batch_index, per_batch):
    return lax.dynamic_slice_in_dim(occ_energy, batch_index * per_batch, per_batch, 0)


def pair_block(
    own_full, own_energy, partner, part_energy, vir_energy, acc_own, acc_part, density, weight
):
    per_batch = own_full.shape[0]

    def one_pair(pair_index, loop_state):
        acc_own, acc_part, density = loop_state
        first_pos = pair_index // per_batch
        second = pair_index % per_batch
        left_block = lax.dynamic_index_in_dim(own_full, first_pos, 0, keepdims=False)
        right_block = lax.dynamic_index_in_dim(partner, second, 0, keepdims=False)
        intersection = lax.dot_general(
            left_block, right_block, (((1,), (1,)), ((), ())), preferred_element_type=jnp.float32
        )
        energy_sum = lax.dynamic_index_in_dim(
            own_energy, first_pos, 0, keepdims=False
        ) + lax.dynamic_index_in_dim(part_energy, second, 0, keepdims=False)
        denominator = energy_sum - vir_energy[:, None] - vir_energy[None, :]
        amplitude = intersection / denominator
        mixed_amp = 2.0 * amplitude - amplitude.T
        amp_half = amplitude.astype(jnp.bfloat16)
        mixed_half = mixed_amp.astype(jnp.bfloat16)
        own_term = jnp.einsum(
            "bp,ab->pa", right_block, mixed_half, preferred_element_type=jnp.float32
        )
        acc_own = acc_own.at[first_pos].add(weight * own_term)
        dens_term = lax.dot_general(
            mixed_half, amp_half, (((1,), (1,)), ((), ())), preferred_element_type=jnp.float32
        )
        part_term = jnp.einsum(
            "ap,ab->pb", left_block, mixed_half, preferred_element_type=jnp.float32
        )
        acc_part = acc_part.at[second].add(weight * part_term)
        dens_term = dens_term + lax.dot_general(
            mixed_half, amp_half, (((0,), (0,)), ((), ())), preferred_element_type=jnp.float32
        )
        density = density + weight * dens_term
        return (acc_own, acc_part, density)

    return lax.fori_loop(0, per_batch * per_batch, one_pair, (acc_own, acc_part, density))


def general_device(factors, occ_energy, vir_energy, metric):
    n_blk = lax.axis_size("blk")
    n_sec = lax.axis_size("sec")
    blk_pos = lax.axis_index("blk")
    sec_pos = lax.axis_index("sec")
    per_batch = factors.shape[0]
    virtuals = factors.shape[1]
    aux_part = factors.shape[2]
    aux_total = aux_part * n_sec
    cycle_turns = min(CYCLE_STEPS, n_blk // (2 * n_sec))
    own_full = lax.all_gather(factors, "sec", axis=2, tiled=True)
    own_energy = batch_energy(occ_energy, blk_pos, per_batch)
    acc_own = jnp.zeros((per_batch, aux_total, virtuals), jnp.float32)
    density = jnp.zeros((virtuals, virtuals), jnp.float32)
    segmented = [factors]
    moving = factors
    for shift_turn in range(n_sec - 1):
        moving = from_behind(moving, "blk", 1)
        segmented.append(moving)
    partner = lax.all_to_all(
        jnp.stack(segmented, 0), "sec", split_axis=0, concat_axis=3, tiled=True
    )[0]
    acc_part = jnp.zeros((per_batch, aux_total, virtuals), jnp.float32)
    for cycle_step in range(cycle_turns):
        if cycle_step > 0:
            partner = from_behind(partner, "blk", n_sec)
            acc_part = from_behind(acc_part, "blk", n_sec)
        offset = sec_pos + n_sec * cycle_step
        weight = jnp.where(offset == 0, jnp.float32(0.5), jnp.float32(1.0))
        part_energy = batch_energy(occ_energy, (blk_pos - offset) % n_blk, per_batch)
        acc_own, acc_part, density = pair_block(
            own_full,
            own_energy,
            partner,
            part_energy,
            vir_energy,
            acc_own,
            acc_part,
            density,
            weight,
        )
    if cycle_turns > 1:
        acc_part = from_behind(acc_part, "blk", -n_sec * (cycle_turns - 1))
    regrouped = lax.all_to_all(acc_part[None], "sec", split_axis=2, concat_axis=0, tiled=True)
    carried = regrouped[n_sec - 1]
    for shift_turn in range(n_sec - 2, -1, -1):
        carried = from_behind(carried, "blk", -1) + regrouped[shift_turn]
    metric_rows = lax.dynamic_slice_in_dim(metric, sec_pos * aux_part, aux_part, 0)
    own_term = jnp.einsum("pq,ipa->qia", metric, acc_own, precision=lax.Precision.HIGHEST)
    gamma_part = lax.psum_scatter(
        own_term + jnp.einsum("pq,ipa->qia", metric_rows, carried, precision=lax.Precision.HIGHEST),
        "sec",
        scatter_dimension=0,
        tiled=True,
    )
    density_rows = lax.psum_scatter(density, "blk", scatter_dimension=0, tiled=True)
    density_out = lax.psum(density_rows, "sec")
    return (gamma_part, density_out)


AXES = ("blk", "sec")
NT = (((1,), (1,)), ((), ()))
NN = (((1,), (0,)), ((), ()))
TAIL_ROWS = 16
VMEM_LIMIT = 16 * 1024 * 1024


def dot(left, right, dims):
    return lax.dot_general(left, right, dims, preferred_element_type=jnp.float32)


def split_bits(device, n_sec):
    blk, sec = device // n_sec, device % n_sec
    return blk // 2, blk % 2, sec // 2, sec % 2


def join_bits(z, y, x, c, n_sec):
    return (2 * z + y) * n_sec + 2 * x + c


def send(value, target, n_blk, n_sec):
    pairs = []
    for device in range(n_blk * n_sec):
        pairs.append((device, join_bits(*target(*split_bits(device, n_sec)), n_sec)))
    return lax.ppermute(value, AXES, pairs)


def encode(value):
    peak = jnp.max(jnp.abs(value), keepdims=True)
    power = jnp.floor(15.4 - jnp.log2(jnp.maximum(peak, 1e-36)))
    power = jnp.clip(power, -120.0, 120.0)
    scaled = value * jnp.exp2(power)
    second = scaled * scaled
    fourth = second * second
    eighth = fourth * fourth
    coded = jnp.where(scaled < 0.0, -eighth, eighth).astype(jnp.bfloat16)
    tail = jnp.broadcast_to(power, (TAIL_ROWS, value.shape[1])).astype(jnp.bfloat16)
    return coded, tail


def encode_into(out, value):
    rows = value.shape[0]
    coded, tail = encode(value)
    out[:rows] = coded
    out[rows:] = tail


def decode(ref):
    rows = ref.shape[0] - TAIL_ROWS
    power = ref[rows:].astype(jnp.float32)[:1]
    coded = ref[:rows].astype(jnp.float32)
    root = jnp.exp2(jnp.log2(jnp.abs(coded)) * 0.125 - power)
    return jnp.where(coded < 0.0, -root, root)


def place_bits():
    blk, sec = lax.axis_index("blk"), lax.axis_index("sec")
    return blk // 2, blk % 2, sec // 2, sec % 2


def pair_terms(occupied, virtual, layer, left, right):
    z, y, x, c = place_bits()
    index = lax.broadcasted_iota(jnp.int32, occupied.shape, 1)

    def energy(batch):
        return jnp.sum(jnp.where(index == batch, occupied[...], 0.0), axis=1, keepdims=True)

    row_energy = virtual[...]
    row_sum = energy(2 * z + c) + energy(2 * layer + y) - row_energy
    col_sum = jnp.broadcast_to(row_sum, (128, row_sum.shape[1])).T[:, :1]
    overlap = dot(left[0], right[0], NT)
    for part in range(1, len(left)):
        overlap += dot(left[part], right[part], NT)
    amplitude = overlap / (col_sum - row_energy)
    return amplitude.astype(jnp.bfloat16), 2.0 * amplitude - amplitude.T


def read_left(refs):
    z, y, x, c = place_bits()
    home = c == y
    own, swapped, near, near_swapped, far, far_swapped = [ref[...] for ref in refs]
    return [
        jnp.where(home, own, near),
        jnp.where(home, swapped, near_swapped),
        jnp.where(home, near, far),
        jnp.where(home, near_swapped, far_swapped),
    ]


def first_pair_kernel(*refs):
    z, y, x, c = place_bits()
    left = read_left(refs[2:8])
    right = [ref[...] for ref in refs[8:12]]
    grad_out, amp_out, mixed_out = refs[-3:]
    layer = jnp.where(x == 1, z, z ^ 1)
    amp_half, mixed = pair_terms(refs[0], refs[1], layer, left, right)
    mixed_half = mixed.astype(jnp.bfloat16)
    width = right[0].shape[1]
    for part in range(4):
        grad_out[:, part * width : (part + 1) * width] = dot(mixed_half, right[part], NN)
    amp_out[...] = amp_half
    mixed_out[...] = mixed_half


def last_pair_kernel(*refs):
    z, y, x, c = place_bits()
    left = read_left(refs[2:8])
    right = [ref[...] for ref in refs[8:12]]
    amp_out, mixed_out = refs[-2:]
    layer = jnp.where(x == 1, z ^ 3, z ^ 2)
    amp_half, mixed = pair_terms(refs[0], refs[1], layer, left, right)
    outside = (x == 0) & (c == y)
    amp_out[...] = amp_half
    mixed_out[...] = jnp.where(outside, 0.0, mixed).astype(jnp.bfloat16)


def density_pairs_kernel(first_amp, first_mixed, last_amp, last_mixed, keep_out, send_out):
    z, y, x, c = place_bits()
    count, rows = keep_out.shape[:2]
    for out, core in ((send_out, c), (keep_out, 1 - c)):
        groups = [
            pl.ds(pl.multiple_of((2 * layer + core) * rows, rows), rows) for layer in range(count)
        ]
        first = jnp.concatenate([first_mixed[group, :] for group in groups], 0)
        last = jnp.concatenate([last_mixed[group, :] for group in groups], 0)
        total = dot(first, first_amp[...], NT) + dot(last, last_amp[...], NT)
        for layer in range(count):
            out[layer] = total[layer * rows : (layer + 1) * rows]


def metric_product(step, metric_high, metric_low, high, low):
    metric_top = metric_high[step]
    block = dot(metric_top, high[...], NT)
    block += dot(metric_top, low[...], NT)
    return block + dot(metric_low[step], high[...], NT)


def gradient_kernel(step, mixed, *refs):
    grad_in, metric_high, metric_low, high_out, low_out, out = refs[4:]
    mixed_half = mixed[...]
    width = refs[0].shape[1]
    for part in range(4):
        cols = slice(part * width, (part + 1) * width)
        grad = grad_in[:, cols] + dot(mixed_half, refs[part][...], NN)
        high = grad.astype(jnp.bfloat16)
        high_out[:, cols] = high
        low_out[:, cols] = (grad - high.astype(jnp.float32)).astype(jnp.bfloat16)
    encode_into(out, metric_product(step, metric_high, metric_low, high_out, low_out))


def metric_kernel(step, metric_high, metric_low, high, low, *refs):
    encode_into(refs[-1], metric_product(step, metric_high, metric_low, high, low))


def turn_metric_kernel(metric, *refs):
    high, low = refs[-2:]
    z, y, x, c = place_bits()
    steps, width, aux_total = high.shape
    row = lax.broadcasted_iota(jnp.int32, (width, width), 0)
    col = lax.broadcasted_iota(jnp.int32, (width, width), 1)
    unit = jnp.where(row == col, 1.0, 0.0).astype(jnp.bfloat16)
    lane = 2 * x + c
    for step in range(steps):
        target = 2 * (x ^ (step >> 1)) + (y ^ (step & 1))
        for part, order in enumerate((lane, lane ^ 2, lane ^ 1, lane ^ 3)):
            value = metric[
                pl.ds(pl.multiple_of(order * width, width), width),
                pl.ds(pl.multiple_of(target * width, width), width),
            ]
            top = value.astype(jnp.bfloat16)
            rest = (value - top.astype(jnp.float32)).astype(jnp.bfloat16)
            cols = slice(part * width, (part + 1) * width)
            high[step, :, cols] = dot(unit, top, NT).astype(jnp.bfloat16)
            low[step, :, cols] = dot(unit, rest, NT).astype(jnp.bfloat16)


def gamma_part_kernel(left, right, *refs):
    refs[-1][...] = decode(left) + decode(right)


def density_cores_kernel(keep, got, *refs):
    layer_out, one, two, three = refs[-4:]
    z, y, x, c = place_bits()
    layer_out[...] = keep[z] + got[z]
    for step, out in enumerate((one, two, three), 1):
        encode_into(out, keep[z ^ step] + got[z ^ step])


def density_rows_kernel(layer, one, two, three, *refs):
    encode_into(refs[-1], layer[...] + decode(one) + decode(two) + decode(three))


def density_block_kernel(far, near, *refs):
    refs[-1][...] = decode(far) + decode(near)


def outcome_kernel(part, left, right, block, other, gamma_out, density_out):
    gamma_out[:, 0, :] = part[...] + decode(left) + decode(right)
    density_out[...] = block[...] + other[...]


def fast_device(factors, occ_energy, vir_energy, metric):
    n_blk = lax.axis_size("blk")
    n_sec = lax.axis_size("sec")
    own = factors[0]
    virtuals, width = own.shape
    aux_total = width * n_sec
    half = virtuals // 2
    rows = virtuals // n_blk
    square = 2 * virtuals * virtuals

    def move(value, target):
        return send(value, target, n_blk, n_sec)

    def core_swap(value):
        return move(value, lambda z, y, x, c: (z, y, x, 1 - c))

    def x_swap(value):
        return move(value, lambda z, y, x, c: (z, y, 1 - x, c))

    def y_swap(value):
        return move(value, lambda z, y, x, c: (z, 1 - y, x, c))

    def xy_swap(value):
        return move(value, lambda z, y, x, c: (z, 1 - y, 1 - x, c))

    def first_partner(value):
        return move(value, lambda z, y, x, c: (z if x else z ^ 1, y, x, c))

    def first_partner_cross(value):
        return move(value, lambda z, y, x, c: (z ^ 1 if x else z, y, 1 - x, c))

    def last_partner(value):
        return move(value, lambda z, y, x, c: (z ^ 3 if x else z ^ 2, y, x, c))

    def last_partner_cross(value):
        return move(value, lambda z, y, x, c: (z ^ 2 if x else z ^ 3, y, 1 - x, c))

    def near_left(value):
        return move(value, lambda z, y, x, c: (z, 1 - y, x, c) if c == y else (z, y, x, 1 - c))

    def far_left(value):
        return move(value, lambda z, y, x, c: (z, y, x, c) if c == y else (z, 1 - y, x, 1 - c))

    vmem = pl.BlockSpec(memory_space=pltpu.VMEM)
    unread = pl.BlockSpec(memory_space=pl.ANY)
    params = pltpu.CompilerParams(vmem_limit_bytes=VMEM_LIMIT)

    def shape(dtype, *dims):
        return jax.ShapeDtypeStruct(dims, dtype)

    def call(name, kernel, outs, operands, earlier=(), scratch=(), flops=0):
        many = isinstance(outs, list)
        with jax.named_scope(name):
            return pl.pallas_call(
                kernel,
                in_specs=[vmem] * len(operands) + [unread] * len(earlier),
                out_specs=[vmem] * len(outs) if many else vmem,
                out_shape=outs,
                scratch_shapes=list(scratch),
                compiler_params=params,
                cost_estimate=pl.CostEstimate(
                    flops=flops,
                    bytes_accessed=0,
                    transcendentals=0,
                ),
            )(*operands, *earlier)

    metric_high, metric_low = call(
        "metric_turn",
        turn_metric_kernel,
        [shape(jnp.bfloat16, n_sec, width, aux_total)] * 2,
        [metric],
        flops=4 * aux_total * aux_total * width,
    )
    with jax.named_scope("gather"):
        swapped = x_swap(own)
        last_own, last_swapped, first_own, first_cross, near_own, far_own, metric_high = lax.optimization_barrier(
            (
                last_partner(own),
                last_partner(swapped),
                first_partner(own),
                first_partner_cross(own),
                near_left(own),
                far_left(own),
                metric_high,
            )
        )
        far_swapped, near_swapped = far_left(swapped), near_left(swapped)
        left = [own, swapped, near_own, near_swapped, far_own, far_swapped]
        first = [first_own, first_cross, core_swap(first_own), core_swap(first_cross)]
        last = [last_own, last_swapped, core_swap(last_own), core_swap(last_swapped)]

    energies = [occ_energy[None, :], vir_energy[None, :]]
    half_square = shape(jnp.bfloat16, virtuals, virtuals)
    grad, first_amp, first_mixed = call(
        "first_pair",
        first_pair_kernel,
        [shape(jnp.float32, virtuals, aux_total), half_square, half_square],
        energies + left + first,
    )
    last_amp, last_mixed = call(
        "last_pair",
        last_pair_kernel,
        [half_square, half_square],
        energies + left + last,
        [first_amp],
        flops=4 * square * aux_total,
    )
    layers = n_blk // 2
    dens_keep, dens_send = call(
        "density_pairs",
        density_pairs_kernel,
        [shape(jnp.float32, layers, rows, virtuals)] * 2,
        [first_amp, first_mixed, last_amp, last_mixed],
        flops=2 * square * virtuals,
    )
    dens_got = core_swap(dens_send)

    message = shape(jnp.bfloat16, width + TAIL_ROWS, virtuals)
    block_flops = 6 * width * virtuals * aux_total
    high, low, third = call(
        "gradient",
        functools.partial(gradient_kernel, 3),
        [
            shape(jnp.bfloat16, virtuals, aux_total),
            shape(jnp.bfloat16, virtuals, aux_total),
            message,
        ],
        [last_mixed, *last, grad, metric_high, metric_low],
        flops=2 * block_flops,
    )

    def gamma_block(step, *earlier):
        return call(
            "gamma_block",
            functools.partial(metric_kernel, step),
            message,
            [metric_high, metric_low, high, low],
            earlier,
            flops=block_flops,
        )

    def gamma_move(step, block):
        return move(block, lambda z, y, x, c: (z, c, x ^ (step >> 1), y ^ (step & 1)))

    def across(value):
        return move(value, lambda z, y, x, c: (z, 1 - c, 1 - x, y))

    def along(value):
        return move(value, lambda z, y, x, c: (z, 1 - c, x, y))

    coded = shape(jnp.bfloat16, rows + TAIL_ROWS, virtuals)
    got_third = gamma_move(3, third)
    layer, *messages = call(
        "density_cores",
        density_cores_kernel,
        [shape(jnp.float32, rows, virtuals)] + [coded] * (layers - 1),
        [dens_keep, dens_got],
        [third],
    )
    got = [
        move(messages[step - 1], lambda z, y, x, c, step=step: (z ^ step, y, x, c))
        for step in range(layers - 1, 0, -1)
    ]
    second = gamma_block(2, messages[0])
    got_second = gamma_move(2, second)
    first_block = gamma_block(1, second)
    got_first = gamma_move(1, first_block)
    partial_rows = call(
        "density_rows",
        density_rows_kernel,
        coded,
        [layer, *got],
        [first_block],
    )
    rows_far, rows_near = across(partial_rows), along(partial_rows)
    zeroth = gamma_block(0, partial_rows)
    got_zeroth = gamma_move(0, zeroth)
    part = call(
        "gamma_part",
        gamma_part_kernel,
        shape(jnp.float32, width, virtuals),
        [got_third, got_second],
        [zeroth, partial_rows],
    )
    block = call(
        "density_block",
        density_block_kernel,
        shape(jnp.float32, rows, virtuals),
        [rows_far, rows_near],
        [part],
    )
    gamma, density = call(
        "outcome",
        outcome_kernel,
        [shape(jnp.float32, width, 1, virtuals), shape(jnp.float32, rows, virtuals)],
        [part, got_first, got_zeroth, block, core_swap(block)],
    )
    return gamma, density


def solution(mesh):
    n_blk, n_sec = mesh.shape["blk"], mesh.shape["sec"]

    def per_device(factors, occ_energy, vir_energy, metric):
        two_rows_of_layers = n_sec == 4 and n_blk == 2 * n_sec and factors.shape[0] == 1
        step = fast_device if two_rows_of_layers else general_device
        return step(factors, occ_energy, vir_energy, metric)

    return jax.shard_map(
        per_device,
        mesh=mesh,
        in_specs=(P("blk", None, "sec"), P(), P(), P()),
        out_specs=(P("sec", "blk", None), P("blk", None)),
        check_vma=False,
    )
```

```python
import functools

import jax
import jax.numpy as jnp
from jax import lax
from jax.experimental import pallas as pl
from jax.experimental.pallas import tpu as pltpu
from jax.sharding import PartitionSpec as P

CYCLE_STEPS = 4


def from_behind(shard, axis, by):
    devices = lax.axis_size(axis)
    return lax.ppermute(shard, axis, [(i, (i + by) % devices) for i in range(devices)])


def batch_energy(occ_energy, batch_index, per_batch):
    return lax.dynamic_slice_in_dim(occ_energy, batch_index * per_batch, per_batch, 0)


def pair_block(
    own_full, own_energy, partner, part_energy, vir_energy, acc_own, acc_part, density, weight
):
    per_batch = own_full.shape[0]

    def one_pair(pair_index, loop_state):
        acc_own, acc_part, density = loop_state
        first_pos = pair_index // per_batch
        second = pair_index % per_batch
        left_block = lax.dynamic_index_in_dim(own_full, first_pos, 0, keepdims=False)
        right_block = lax.dynamic_index_in_dim(partner, second, 0, keepdims=False)
        intersection = lax.dot_general(
            left_block, right_block, (((1,), (1,)), ((), ())), preferred_element_type=jnp.float32
        )
        energy_sum = lax.dynamic_index_in_dim(
            own_energy, first_pos, 0, keepdims=False
        ) + lax.dynamic_index_in_dim(part_energy, second, 0, keepdims=False)
        denominator = energy_sum - vir_energy[:, None] - vir_energy[None, :]
        amplitude = intersection / denominator
        mixed_amp = 2.0 * amplitude - amplitude.T
        amp_half = amplitude.astype(jnp.bfloat16)
        mixed_half = mixed_amp.astype(jnp.bfloat16)
        own_term = jnp.einsum(
            "bp,ab->pa", right_block, mixed_half, preferred_element_type=jnp.float32
        )
        acc_own = acc_own.at[first_pos].add(weight * own_term)
        dens_term = lax.dot_general(
            mixed_half, amp_half, (((1,), (1,)), ((), ())), preferred_element_type=jnp.float32
        )
        part_term = jnp.einsum(
            "ap,ab->pb", left_block, mixed_half, preferred_element_type=jnp.float32
        )
        acc_part = acc_part.at[second].add(weight * part_term)
        dens_term = dens_term + lax.dot_general(
            mixed_half, amp_half, (((0,), (0,)), ((), ())), preferred_element_type=jnp.float32
        )
        density = density + weight * dens_term
        return (acc_own, acc_part, density)

    return lax.fori_loop(0, per_batch * per_batch, one_pair, (acc_own, acc_part, density))


def general_device(factors, occ_energy, vir_energy, metric):
    n_blk = lax.axis_size("blk")
    n_sec = lax.axis_size("sec")
    blk_pos = lax.axis_index("blk")
    sec_pos = lax.axis_index("sec")
    per_batch = factors.shape[0]
    virtuals = factors.shape[1]
    aux_part = factors.shape[2]
    aux_total = aux_part * n_sec
    cycle_turns = min(CYCLE_STEPS, n_blk // (2 * n_sec))
    own_full = lax.all_gather(factors, "sec", axis=2, tiled=True)
    own_energy = batch_energy(occ_energy, blk_pos, per_batch)
    acc_own = jnp.zeros((per_batch, aux_total, virtuals), jnp.float32)
    density = jnp.zeros((virtuals, virtuals), jnp.float32)
    segmented = [factors]
    moving = factors
    for shift_turn in range(n_sec - 1):
        moving = from_behind(moving, "blk", 1)
        segmented.append(moving)
    partner = lax.all_to_all(
        jnp.stack(segmented, 0), "sec", split_axis=0, concat_axis=3, tiled=True
    )[0]
    acc_part = jnp.zeros((per_batch, aux_total, virtuals), jnp.float32)
    for cycle_step in range(cycle_turns):
        if cycle_step > 0:
            partner = from_behind(partner, "blk", n_sec)
            acc_part = from_behind(acc_part, "blk", n_sec)
        offset = sec_pos + n_sec * cycle_step
        weight = jnp.where(offset == 0, jnp.float32(0.5), jnp.float32(1.0))
        part_energy = batch_energy(occ_energy, (blk_pos - offset) % n_blk, per_batch)
        acc_own, acc_part, density = pair_block(
            own_full,
            own_energy,
            partner,
            part_energy,
            vir_energy,
            acc_own,
            acc_part,
            density,
            weight,
        )
    if cycle_turns > 1:
        acc_part = from_behind(acc_part, "blk", -n_sec * (cycle_turns - 1))
    regrouped = lax.all_to_all(acc_part[None], "sec", split_axis=2, concat_axis=0, tiled=True)
    carried = regrouped[n_sec - 1]
    for shift_turn in range(n_sec - 2, -1, -1):
        carried = from_behind(carried, "blk", -1) + regrouped[shift_turn]
    metric_rows = lax.dynamic_slice_in_dim(metric, sec_pos * aux_part, aux_part, 0)
    own_term = jnp.einsum("pq,ipa->qia", metric, acc_own, precision=lax.Precision.HIGHEST)
    gamma_part = lax.psum_scatter(
        own_term + jnp.einsum("pq,ipa->qia", metric_rows, carried, precision=lax.Precision.HIGHEST),
        "sec",
        scatter_dimension=0,
        tiled=True,
    )
    density_rows = lax.psum_scatter(density, "blk", scatter_dimension=0, tiled=True)
    density_out = lax.psum(density_rows, "sec")
    return (gamma_part, density_out)


AXES = ("blk", "sec")
NT = (((1,), (1,)), ((), ()))
NN = (((1,), (0,)), ((), ()))
TAIL_ROWS = 16
VMEM_LIMIT = 16 * 1024 * 1024


def dot(left, right, dims):
    return lax.dot_general(left, right, dims, preferred_element_type=jnp.float32)


def split_bits(device, n_sec):
    blk, sec = device // n_sec, device % n_sec
    return blk // 2, blk % 2, sec // 2, sec % 2


def join_bits(z, y, x, c, n_sec):
    return (2 * z + y) * n_sec + 2 * x + c


def send(value, target, n_blk, n_sec):
    pairs = []
    for device in range(n_blk * n_sec):
        pairs.append((device, join_bits(*target(*split_bits(device, n_sec)), n_sec)))
    return lax.ppermute(value, AXES, pairs)


def encode(value):
    peak = jnp.max(jnp.abs(value), keepdims=True)
    power = jnp.floor(15.4 - jnp.log2(jnp.maximum(peak, 1e-36)))
    power = jnp.clip(power, -120.0, 120.0)
    scaled = value * jnp.exp2(power)
    second = scaled * scaled
    fourth = second * second
    eighth = fourth * fourth
    coded = jnp.where(scaled < 0.0, -eighth, eighth).astype(jnp.bfloat16)
    tail = jnp.broadcast_to(power, (TAIL_ROWS, value.shape[1])).astype(jnp.bfloat16)
    return coded, tail


def encode_into(out, value):
    rows = value.shape[0]
    coded, tail = encode(value)
    out[:rows] = coded
    out[rows:] = tail


def decode(ref):
    rows = ref.shape[0] - TAIL_ROWS
    power = ref[rows:].astype(jnp.float32)[:1]
    coded = ref[:rows].astype(jnp.float32)
    root = jnp.exp2(jnp.log2(jnp.abs(coded)) * 0.125 - power)
    return jnp.where(coded < 0.0, -root, root)


def place_bits():
    blk, sec = lax.axis_index("blk"), lax.axis_index("sec")
    return blk // 2, blk % 2, sec // 2, sec % 2


def pair_terms(occupied, virtual, layer, overlap):
    z, y, x, c = place_bits()
    index = lax.broadcasted_iota(jnp.int32, occupied.shape, 1)

    def energy(batch):
        return jnp.sum(jnp.where(index == batch, occupied[...], 0.0), axis=1, keepdims=True)

    row_energy = virtual[...]
    row_sum = energy(2 * z + c) + energy(2 * layer + y) - row_energy
    col_sum = jnp.broadcast_to(row_sum, (128, row_sum.shape[1])).T[:, :1]
    amplitude = overlap / (col_sum - row_energy)
    return amplitude.astype(jnp.bfloat16), 2.0 * amplitude - amplitude.T


def half_overlap_kernel(own, swapped, near, near_swapped, *refs):
    z, y, x, c = place_bits()
    home = c == y
    left = jnp.where(home, own[...], near[...])
    left_swapped = jnp.where(home, swapped[...], near_swapped[...])
    for pair in range(2):
        right, right_swapped = refs[2 * pair], refs[2 * pair + 1]
        refs[4 + pair][...] = dot(left, right[...], NT) + dot(left_swapped, right_swapped[...], NT)


def whole_overlap(half, lefts, rights):
    z, y, x, c = place_bits()
    home = c == y
    near, near_swapped, far, far_swapped = [ref[...] for ref in lefts]
    right, right_swapped = [ref[...] for ref in rights]
    left = jnp.where(home, near, far)
    left_swapped = jnp.where(home, near_swapped, far_swapped)
    return half[...] + dot(left, right, NT) + dot(left_swapped, right_swapped, NT)


def first_pair_kernel(occupied, virtual, half, *refs):
    z, y, x, c = place_bits()
    overlap = whole_overlap(half, refs[:4], refs[6:8])
    grad_out, amp_out, mixed_out = refs[-3:]
    layer = jnp.where(x == 1, z, z ^ 1)
    amp_half, mixed = pair_terms(occupied, virtual, layer, overlap)
    mixed_half = mixed.astype(jnp.bfloat16)
    width = refs[4].shape[1]
    for part, right in enumerate(refs[4:8]):
        grad_out[:, part * width : (part + 1) * width] = dot(mixed_half, right[...], NN)
    amp_out[...] = amp_half
    mixed_out[...] = mixed_half


def last_pair_kernel(occupied, virtual, half, *refs):
    z, y, x, c = place_bits()
    overlap = whole_overlap(half, refs[:4], refs[4:6])
    amp_out, mixed_out = refs[-2:]
    layer = jnp.where(x == 1, z ^ 3, z ^ 2)
    amp_half, mixed = pair_terms(occupied, virtual, layer, overlap)
    outside = (x == 0) & (c == y)
    amp_out[...] = amp_half
    mixed_out[...] = jnp.where(outside, 0.0, mixed).astype(jnp.bfloat16)


def density_pairs_kernel(first_amp, first_mixed, last_amp, last_mixed, keep_out, send_out):
    z, y, x, c = place_bits()
    count, rows = keep_out.shape[:2]
    for out, core in ((send_out, c), (keep_out, 1 - c)):
        groups = [
            pl.ds(pl.multiple_of((2 * layer + core) * rows, rows), rows) for layer in range(count)
        ]
        first = jnp.concatenate([first_mixed[group, :] for group in groups], 0)
        last = jnp.concatenate([last_mixed[group, :] for group in groups], 0)
        total = dot(first, first_amp[...], NT) + dot(last, last_amp[...], NT)
        for layer in range(count):
            out[layer] = total[layer * rows : (layer + 1) * rows]


def metric_product(step, metric_high, metric_low, high, low):
    metric_top = metric_high[step]
    block = dot(metric_top, high[...], NT)
    block += dot(metric_top, low[...], NT)
    return block + dot(metric_low[step], high[...], NT)


def gradient_kernel(step, mixed, *refs):
    grad_in, metric_high, metric_low, high_out, low_out, out = refs[4:]
    mixed_half = mixed[...]
    width = refs[0].shape[1]
    for part in range(4):
        cols = slice(part * width, (part + 1) * width)
        grad = grad_in[:, cols] + dot(mixed_half, refs[part][...], NN)
        high = grad.astype(jnp.bfloat16)
        high_out[:, cols] = high
        low_out[:, cols] = (grad - high.astype(jnp.float32)).astype(jnp.bfloat16)
    encode_into(out, metric_product(step, metric_high, metric_low, high_out, low_out))


def metric_kernel(step, metric_high, metric_low, high, low, *refs):
    encode_into(refs[-1], metric_product(step, metric_high, metric_low, high, low))


def turn_metric_kernel(metric, *refs):
    high, low = refs[-2:]
    z, y, x, c = place_bits()
    steps, width, aux_total = high.shape
    row = lax.broadcasted_iota(jnp.int32, (width, width), 0)
    col = lax.broadcasted_iota(jnp.int32, (width, width), 1)
    unit = jnp.where(row == col, 1.0, 0.0).astype(jnp.bfloat16)
    lane = 2 * x + c
    for step in range(steps):
        target = 2 * (x ^ (step >> 1)) + (y ^ (step & 1))
        for part, order in enumerate((lane, lane ^ 2, lane ^ 1, lane ^ 3)):
            value = metric[
                pl.ds(pl.multiple_of(order * width, width), width),
                pl.ds(pl.multiple_of(target * width, width), width),
            ]
            top = value.astype(jnp.bfloat16)
            rest = (value - top.astype(jnp.float32)).astype(jnp.bfloat16)
            cols = slice(part * width, (part + 1) * width)
            high[step, :, cols] = dot(unit, top, NT).astype(jnp.bfloat16)
            low[step, :, cols] = dot(unit, rest, NT).astype(jnp.bfloat16)


def gamma_part_kernel(left, right, *refs):
    refs[-1][...] = decode(left) + decode(right)


def density_cores_kernel(keep, got, *refs):
    layer_out, one, two, three = refs[-4:]
    z, y, x, c = place_bits()
    layer_out[...] = keep[z] + got[z]
    for step, out in enumerate((one, two, three), 1):
        encode_into(out, keep[z ^ step] + got[z ^ step])


def density_rows_kernel(layer, one, two, three, *refs):
    encode_into(refs[-1], layer[...] + decode(one) + decode(two) + decode(three))


def density_block_kernel(far, near, *refs):
    refs[-1][...] = decode(far) + decode(near)


def gamma_sum_kernel(part, left, right, *refs):
    refs[-1][:, 0, :] = part[...] + decode(left) + decode(right)


def density_sum_kernel(block, other, *refs):
    refs[-1][...] = block[...] + other[...]


def fast_device(factors, occ_energy, vir_energy, metric):
    n_blk = lax.axis_size("blk")
    n_sec = lax.axis_size("sec")
    own = factors[0]
    virtuals, width = own.shape
    aux_total = width * n_sec
    half = virtuals // 2
    rows = virtuals // n_blk
    square = 2 * virtuals * virtuals

    def move(value, target):
        return send(value, target, n_blk, n_sec)

    def core_swap(value):
        return move(value, lambda z, y, x, c: (z, y, x, 1 - c))

    def x_swap(value):
        return move(value, lambda z, y, x, c: (z, y, 1 - x, c))

    def y_swap(value):
        return move(value, lambda z, y, x, c: (z, 1 - y, x, c))

    def xy_swap(value):
        return move(value, lambda z, y, x, c: (z, 1 - y, 1 - x, c))

    def first_partner(value):
        return move(value, lambda z, y, x, c: (z if x else z ^ 1, y, x, c))

    def first_partner_cross(value):
        return move(value, lambda z, y, x, c: (z ^ 1 if x else z, y, 1 - x, c))

    def last_partner(value):
        return move(value, lambda z, y, x, c: (z ^ 3 if x else z ^ 2, y, x, c))

    def last_partner_cross(value):
        return move(value, lambda z, y, x, c: (z ^ 2 if x else z ^ 3, y, 1 - x, c))

    def near_left(value):
        return move(value, lambda z, y, x, c: (z, 1 - y, x, c) if c == y else (z, y, x, 1 - c))

    def far_left(value):
        return move(value, lambda z, y, x, c: (z, y, x, c) if c == y else (z, 1 - y, x, 1 - c))

    vmem = pl.BlockSpec(memory_space=pltpu.VMEM)
    unread = pl.BlockSpec(memory_space=pl.ANY)
    params = pltpu.CompilerParams(vmem_limit_bytes=VMEM_LIMIT)

    def shape(dtype, *dims):
        return jax.ShapeDtypeStruct(dims, dtype)

    def call(name, kernel, outs, operands, earlier=(), scratch=(), flops=0):
        many = isinstance(outs, list)
        with jax.named_scope(name):
            return pl.pallas_call(
                kernel,
                in_specs=[vmem] * len(operands) + [unread] * len(earlier),
                out_specs=[vmem] * len(outs) if many else vmem,
                out_shape=outs,
                scratch_shapes=list(scratch),
                compiler_params=params,
                cost_estimate=pl.CostEstimate(
                    flops=flops,
                    bytes_accessed=0,
                    transcendentals=0,
                ),
            )(*operands, *earlier)

    metric_high, metric_low = call(
        "metric_turn",
        turn_metric_kernel,
        [shape(jnp.bfloat16, n_sec, width, aux_total)] * 2,
        [metric],
        flops=4 * aux_total * aux_total * width,
    )
    with jax.named_scope("gather"):
        swapped = x_swap(own)
        last_own, last_swapped, first_own, first_cross, near_own, far_own, metric_high = lax.optimization_barrier(
            (
                last_partner(own),
                last_partner(swapped),
                first_partner(own),
                first_partner_cross(own),
                near_left(own),
                far_left(own),
                metric_high,
            )
        )
        far_swapped, near_swapped = far_left(swapped), near_left(swapped)
        left = [own, swapped, near_own, near_swapped, far_own, far_swapped]
        first = [first_own, first_cross, core_swap(first_own), core_swap(first_cross)]
        last = [last_own, last_swapped, core_swap(last_own), core_swap(last_swapped)]

    energies = [occ_energy[None, :], vir_energy[None, :]]
    first_half, last_half = call(
        "half_overlap",
        half_overlap_kernel,
        [shape(jnp.float32, virtuals, virtuals)] * 2,
        [*left[:4], *first[:2], *last[:2]],
        flops=2 * square * aux_total,
    )
    half_square = shape(jnp.bfloat16, virtuals, virtuals)
    grad, first_amp, first_mixed = call(
        "first_pair",
        first_pair_kernel,
        [shape(jnp.float32, virtuals, aux_total), half_square, half_square],
        [*energies, first_half, *left[2:], *first],
    )
    last_amp, last_mixed = call(
        "last_pair",
        last_pair_kernel,
        [half_square, half_square],
        [*energies, last_half, *left[2:], *last[2:]],
        [first_amp],
        flops=4 * square * aux_total,
    )
    layers = n_blk // 2
    dens_keep, dens_send = call(
        "density_pairs",
        density_pairs_kernel,
        [shape(jnp.float32, layers, rows, virtuals)] * 2,
        [first_amp, first_mixed, last_amp, last_mixed],
        flops=2 * square * virtuals,
    )
    dens_got = core_swap(dens_send)

    message = shape(jnp.bfloat16, width + TAIL_ROWS, virtuals)
    block_flops = 6 * width * virtuals * aux_total
    high, low, third = call(
        "gradient",
        functools.partial(gradient_kernel, 3),
        [
            shape(jnp.bfloat16, virtuals, aux_total),
            shape(jnp.bfloat16, virtuals, aux_total),
            message,
        ],
        [last_mixed, *last, grad, metric_high, metric_low],
        flops=2 * block_flops,
    )

    def gamma_block(step, *earlier):
        return call(
            "gamma_block",
            functools.partial(metric_kernel, step),
            message,
            [metric_high, metric_low, high, low],
            earlier,
            flops=block_flops,
        )

    def gamma_move(step, block):
        return move(block, lambda z, y, x, c: (z, c, x ^ (step >> 1), y ^ (step & 1)))

    def across(value):
        return move(value, lambda z, y, x, c: (z, 1 - c, 1 - x, y))

    def along(value):
        return move(value, lambda z, y, x, c: (z, 1 - c, x, y))

    coded = shape(jnp.bfloat16, rows + TAIL_ROWS, virtuals)
    got_third = gamma_move(3, third)
    layer, *messages = call(
        "density_cores",
        density_cores_kernel,
        [shape(jnp.float32, rows, virtuals)] + [coded] * (layers - 1),
        [dens_keep, dens_got],
        [third],
    )
    got = [
        move(messages[step - 1], lambda z, y, x, c, step=step: (z ^ step, y, x, c))
        for step in range(layers - 1, 0, -1)
    ]
    second = gamma_block(2, messages[0])
    got_second = gamma_move(2, second)
    first_block = gamma_block(1, second)
    got_first = gamma_move(1, first_block)
    partial_rows = call(
        "density_rows",
        density_rows_kernel,
        coded,
        [layer, *got],
        [first_block],
    )
    rows_far, rows_near = across(partial_rows), along(partial_rows)
    zeroth = gamma_block(0, partial_rows)
    got_zeroth = gamma_move(0, zeroth)
    part = call(
        "gamma_part",
        gamma_part_kernel,
        shape(jnp.float32, width, virtuals),
        [got_third, got_second],
        [zeroth, partial_rows],
    )
    block = call(
        "density_block",
        density_block_kernel,
        shape(jnp.float32, rows, virtuals),
        [rows_far, rows_near],
        [part],
    )
    other = core_swap(block)
    gamma = call(
        "gamma_sum",
        gamma_sum_kernel,
        shape(jnp.float32, width, 1, virtuals),
        [part, got_first, got_zeroth],
        [block],
    )
    density = call(
        "density_sum",
        density_sum_kernel,
        shape(jnp.float32, rows, virtuals),
        [block, other],
    )
    return gamma, density


def solution(mesh):
    n_blk, n_sec = mesh.shape["blk"], mesh.shape["sec"]

    def per_device(factors, occ_energy, vir_energy, metric):
        two_rows_of_layers = n_sec == 4 and n_blk == 2 * n_sec and factors.shape[0] == 1
        step = fast_device if two_rows_of_layers else general_device
        return step(factors, occ_energy, vir_energy, metric)

    return jax.shard_map(
        per_device,
        mesh=mesh,
        in_specs=(P("blk", None, "sec"), P(), P(), P()),
        out_specs=(P("sec", "blk", None), P("blk", None)),
        check_vma=False,
    )
```

```python
import functools

import jax
import jax.numpy as jnp
from jax import lax
from jax.experimental import pallas as pl
from jax.experimental.pallas import tpu as pltpu
from jax.sharding import PartitionSpec as P

CYCLE_STEPS = 4


def from_behind(shard, axis, by):
    devices = lax.axis_size(axis)
    return lax.ppermute(shard, axis, [(i, (i + by) % devices) for i in range(devices)])


def batch_energy(occ_energy, batch_index, per_batch):
    return lax.dynamic_slice_in_dim(occ_energy, batch_index * per_batch, per_batch, 0)


def pair_block(
    own_full, own_energy, partner, part_energy, vir_energy, acc_own, acc_part, density, weight
):
    per_batch = own_full.shape[0]

    def one_pair(pair_index, loop_state):
        acc_own, acc_part, density = loop_state
        first_pos = pair_index // per_batch
        second = pair_index % per_batch
        left_block = lax.dynamic_index_in_dim(own_full, first_pos, 0, keepdims=False)
        right_block = lax.dynamic_index_in_dim(partner, second, 0, keepdims=False)
        intersection = lax.dot_general(
            left_block, right_block, (((1,), (1,)), ((), ())), preferred_element_type=jnp.float32
        )
        energy_sum = lax.dynamic_index_in_dim(
            own_energy, first_pos, 0, keepdims=False
        ) + lax.dynamic_index_in_dim(part_energy, second, 0, keepdims=False)
        denominator = energy_sum - vir_energy[:, None] - vir_energy[None, :]
        amplitude = intersection / denominator
        mixed_amp = 2.0 * amplitude - amplitude.T
        amp_half = amplitude.astype(jnp.bfloat16)
        mixed_half = mixed_amp.astype(jnp.bfloat16)
        own_term = jnp.einsum(
            "bp,ab->pa", right_block, mixed_half, preferred_element_type=jnp.float32
        )
        acc_own = acc_own.at[first_pos].add(weight * own_term)
        dens_term = lax.dot_general(
            mixed_half, amp_half, (((1,), (1,)), ((), ())), preferred_element_type=jnp.float32
        )
        part_term = jnp.einsum(
            "ap,ab->pb", left_block, mixed_half, preferred_element_type=jnp.float32
        )
        acc_part = acc_part.at[second].add(weight * part_term)
        dens_term = dens_term + lax.dot_general(
            mixed_half, amp_half, (((0,), (0,)), ((), ())), preferred_element_type=jnp.float32
        )
        density = density + weight * dens_term
        return (acc_own, acc_part, density)

    return lax.fori_loop(0, per_batch * per_batch, one_pair, (acc_own, acc_part, density))


def general_device(factors, occ_energy, vir_energy, metric):
    n_blk = lax.axis_size("blk")
    n_sec = lax.axis_size("sec")
    blk_pos = lax.axis_index("blk")
    sec_pos = lax.axis_index("sec")
    per_batch = factors.shape[0]
    virtuals = factors.shape[1]
    aux_part = factors.shape[2]
    aux_total = aux_part * n_sec
    cycle_turns = min(CYCLE_STEPS, n_blk // (2 * n_sec))
    own_full = lax.all_gather(factors, "sec", axis=2, tiled=True)
    own_energy = batch_energy(occ_energy, blk_pos, per_batch)
    acc_own = jnp.zeros((per_batch, aux_total, virtuals), jnp.float32)
    density = jnp.zeros((virtuals, virtuals), jnp.float32)
    segmented = [factors]
    moving = factors
    for shift_turn in range(n_sec - 1):
        moving = from_behind(moving, "blk", 1)
        segmented.append(moving)
    partner = lax.all_to_all(
        jnp.stack(segmented, 0), "sec", split_axis=0, concat_axis=3, tiled=True
    )[0]
    acc_part = jnp.zeros((per_batch, aux_total, virtuals), jnp.float32)
    for cycle_step in range(cycle_turns):
        if cycle_step > 0:
            partner = from_behind(partner, "blk", n_sec)
            acc_part = from_behind(acc_part, "blk", n_sec)
        offset = sec_pos + n_sec * cycle_step
        weight = jnp.where(offset == 0, jnp.float32(0.5), jnp.float32(1.0))
        part_energy = batch_energy(occ_energy, (blk_pos - offset) % n_blk, per_batch)
        acc_own, acc_part, density = pair_block(
            own_full,
            own_energy,
            partner,
            part_energy,
            vir_energy,
            acc_own,
            acc_part,
            density,
            weight,
        )
    if cycle_turns > 1:
        acc_part = from_behind(acc_part, "blk", -n_sec * (cycle_turns - 1))
    regrouped = lax.all_to_all(acc_part[None], "sec", split_axis=2, concat_axis=0, tiled=True)
    carried = regrouped[n_sec - 1]
    for shift_turn in range(n_sec - 2, -1, -1):
        carried = from_behind(carried, "blk", -1) + regrouped[shift_turn]
    metric_rows = lax.dynamic_slice_in_dim(metric, sec_pos * aux_part, aux_part, 0)
    own_term = jnp.einsum("pq,ipa->qia", metric, acc_own, precision=lax.Precision.HIGHEST)
    gamma_part = lax.psum_scatter(
        own_term + jnp.einsum("pq,ipa->qia", metric_rows, carried, precision=lax.Precision.HIGHEST),
        "sec",
        scatter_dimension=0,
        tiled=True,
    )
    density_rows = lax.psum_scatter(density, "blk", scatter_dimension=0, tiled=True)
    density_out = lax.psum(density_rows, "sec")
    return (gamma_part, density_out)


AXES = ("blk", "sec")
NT = (((1,), (1,)), ((), ()))
NN = (((1,), (0,)), ((), ()))
TAIL_ROWS = 16
VMEM_LIMIT = 16 * 1024 * 1024


def dot(left, right, dims):
    return lax.dot_general(left, right, dims, preferred_element_type=jnp.float32)


def split_bits(device, n_sec):
    blk, sec = device // n_sec, device % n_sec
    return blk // 2, blk % 2, sec // 2, sec % 2


def join_bits(z, y, x, c, n_sec):
    return (2 * z + y) * n_sec + 2 * x + c


def send(value, target, n_blk, n_sec):
    pairs = []
    for device in range(n_blk * n_sec):
        pairs.append((device, join_bits(*target(*split_bits(device, n_sec)), n_sec)))
    return lax.ppermute(value, AXES, pairs)


def encode(value):
    peak = jnp.max(jnp.abs(value), keepdims=True)
    power = jnp.floor(15.4 - jnp.log2(jnp.maximum(peak, 1e-36)))
    power = jnp.clip(power, -120.0, 120.0)
    scaled = value * jnp.exp2(power)
    second = scaled * scaled
    fourth = second * second
    eighth = fourth * fourth
    coded = jnp.where(scaled < 0.0, -eighth, eighth).astype(jnp.bfloat16)
    tail = jnp.broadcast_to(power, (TAIL_ROWS, value.shape[1])).astype(jnp.bfloat16)
    return coded, tail


def encode_into(out, value):
    rows = value.shape[0]
    coded, tail = encode(value)
    out[:rows] = coded
    out[rows:] = tail


def decode(ref):
    rows = ref.shape[0] - TAIL_ROWS
    power = ref[rows:].astype(jnp.float32)[:1]
    coded = ref[:rows].astype(jnp.float32)
    root = jnp.exp2(jnp.log2(jnp.abs(coded)) * 0.125 - power)
    return jnp.where(coded < 0.0, -root, root)


def place_bits():
    blk, sec = lax.axis_index("blk"), lax.axis_index("sec")
    return blk // 2, blk % 2, sec // 2, sec % 2


def pair_terms(occupied, virtual, layer, overlap):
    z, y, x, c = place_bits()
    index = lax.broadcasted_iota(jnp.int32, occupied.shape, 1)

    def energy(batch):
        return jnp.sum(jnp.where(index == batch, occupied[...], 0.0), axis=1, keepdims=True)

    row_energy = virtual[...]
    row_sum = energy(2 * z + c) + energy(2 * layer + y) - row_energy
    col_sum = jnp.broadcast_to(row_sum, (128, row_sum.shape[1])).T[:, :1]
    amplitude = overlap / (col_sum - row_energy)
    return amplitude.astype(jnp.bfloat16), 2.0 * amplitude - amplitude.T


def half_overlap_kernel(own, swapped, near, near_swapped, *refs):
    z, y, x, c = place_bits()
    home = c == y
    left = jnp.where(home, own[...], near[...])
    left_swapped = jnp.where(home, swapped[...], near_swapped[...])
    for pair in range(2):
        right, right_swapped = refs[2 * pair], refs[2 * pair + 1]
        refs[4 + pair][...] = dot(left, right[...], NT) + dot(left_swapped, right_swapped[...], NT)


def whole_overlap(half, lefts, rights):
    z, y, x, c = place_bits()
    home = c == y
    near, near_swapped, far, far_swapped = [ref[...] for ref in lefts]
    right, right_swapped = [ref[...] for ref in rights]
    left = jnp.where(home, near, far)
    left_swapped = jnp.where(home, near_swapped, far_swapped)
    return half[...] + dot(left, right, NT) + dot(left_swapped, right_swapped, NT)


def first_pair_kernel(occupied, virtual, half, *refs):
    z, y, x, c = place_bits()
    overlap = whole_overlap(half, refs[:4], refs[6:8])
    grad_out, amp_out, mixed_out = refs[-3:]
    layer = jnp.where(x == 1, z, z ^ 1)
    amp_half, mixed = pair_terms(occupied, virtual, layer, overlap)
    mixed_half = mixed.astype(jnp.bfloat16)
    width = refs[4].shape[1]
    for part, right in enumerate(refs[4:8]):
        grad_out[:, part * width : (part + 1) * width] = dot(mixed_half, right[...], NN)
    amp_out[...] = amp_half
    mixed_out[...] = mixed_half


def last_pair_kernel(occupied, virtual, half, *refs):
    z, y, x, c = place_bits()
    overlap = whole_overlap(half, refs[:4], refs[4:6])
    amp_out, mixed_out = refs[-2:]
    layer = jnp.where(x == 1, z ^ 3, z ^ 2)
    amp_half, mixed = pair_terms(occupied, virtual, layer, overlap)
    outside = (x == 0) & (c == y)
    amp_out[...] = amp_half
    mixed_out[...] = jnp.where(outside, 0.0, mixed).astype(jnp.bfloat16)


def density_pairs_kernel(first_amp, first_mixed, last_amp, last_mixed, keep_out, send_out):
    z, y, x, c = place_bits()
    count, rows = keep_out.shape[:2]
    for out, core in ((send_out, c), (keep_out, 1 - c)):
        groups = [
            pl.ds(pl.multiple_of((2 * layer + core) * rows, rows), rows) for layer in range(count)
        ]
        first = jnp.concatenate([first_mixed[group, :] for group in groups], 0)
        last = jnp.concatenate([last_mixed[group, :] for group in groups], 0)
        total = dot(first, first_amp[...], NT) + dot(last, last_amp[...], NT)
        for layer in range(count):
            out[layer] = total[layer * rows : (layer + 1) * rows]


def metric_product(step, metric_high, metric_low, high, low):
    metric_top = metric_high[step]
    block = dot(metric_top, high[...], NT)
    block += dot(metric_top, low[...], NT)
    return block + dot(metric_low[step], high[...], NT)


def gradient_kernel(step, mixed, *refs):
    grad_in, metric_high, metric_low, high_out, low_out, out = refs[4:]
    mixed_half = mixed[...]
    width = refs[0].shape[1]
    for part in range(4):
        cols = slice(part * width, (part + 1) * width)
        grad = grad_in[:, cols] + dot(mixed_half, refs[part][...], NN)
        high = grad.astype(jnp.bfloat16)
        high_out[:, cols] = high
        low_out[:, cols] = (grad - high.astype(jnp.float32)).astype(jnp.bfloat16)
    encode_into(out, metric_product(step, metric_high, metric_low, high_out, low_out))


def metric_kernel(step, metric_high, metric_low, high, low, *refs):
    encode_into(refs[-1], metric_product(step, metric_high, metric_low, high, low))


def turn_metric_kernel(metric, *refs):
    high, low = refs[-2:]
    z, y, x, c = place_bits()
    steps, width, aux_total = high.shape
    row = lax.broadcasted_iota(jnp.int32, (width, width), 0)
    col = lax.broadcasted_iota(jnp.int32, (width, width), 1)
    unit = jnp.where(row == col, 1.0, 0.0).astype(jnp.bfloat16)
    lane = 2 * x + c
    for step in range(steps):
        target = 2 * (x ^ (step >> 1)) + (y ^ (step & 1))
        for part, order in enumerate((lane, lane ^ 2, lane ^ 1, lane ^ 3)):
            value = metric[
                pl.ds(pl.multiple_of(order * width, width), width),
                pl.ds(pl.multiple_of(target * width, width), width),
            ]
            top = value.astype(jnp.bfloat16)
            rest = (value - top.astype(jnp.float32)).astype(jnp.bfloat16)
            cols = slice(part * width, (part + 1) * width)
            high[step, :, cols] = dot(unit, top, NT).astype(jnp.bfloat16)
            low[step, :, cols] = dot(unit, rest, NT).astype(jnp.bfloat16)


def decode_kernel(message, *refs):
    refs[-1][...] = decode(message)


def gamma_part_kernel(part, message, *refs):
    refs[-1][...] = part[...] + decode(message)


def density_cores_kernel(keep, got, *refs):
    layer_out, one, two, three = refs[-4:]
    z, y, x, c = place_bits()
    layer_out[...] = keep[z] + got[z]
    for step, out in enumerate((one, two, three), 1):
        encode_into(out, keep[z ^ step] + got[z ^ step])


def density_rows_kernel(layer, one, two, three, *refs):
    encode_into(refs[-1], layer[...] + decode(one) + decode(two) + decode(three))


def density_block_kernel(far, near, *refs):
    refs[-1][...] = decode(far) + decode(near)


def gamma_sum_kernel(part, left, right, *refs):
    refs[-1][:, 0, :] = part[...] + decode(left) + decode(right)


def density_sum_kernel(block, other, *refs):
    refs[-1][...] = block[...] + other[...]


def fast_device(factors, occ_energy, vir_energy, metric):
    n_blk = lax.axis_size("blk")
    n_sec = lax.axis_size("sec")
    own = factors[0]
    virtuals, width = own.shape
    aux_total = width * n_sec
    half = virtuals // 2
    rows = virtuals // n_blk
    square = 2 * virtuals * virtuals

    def move(value, target):
        return send(value, target, n_blk, n_sec)

    def core_swap(value):
        return move(value, lambda z, y, x, c: (z, y, x, 1 - c))

    def x_swap(value):
        return move(value, lambda z, y, x, c: (z, y, 1 - x, c))

    def y_swap(value):
        return move(value, lambda z, y, x, c: (z, 1 - y, x, c))

    def xy_swap(value):
        return move(value, lambda z, y, x, c: (z, 1 - y, 1 - x, c))

    def first_partner(value):
        return move(value, lambda z, y, x, c: (z if x else z ^ 1, y, x, c))

    def first_partner_cross(value):
        return move(value, lambda z, y, x, c: (z ^ 1 if x else z, y, 1 - x, c))

    def opposite_layer(value):
        return move(value, lambda z, y, x, c: (z ^ 2, y, x, c))

    def last_forward(value):
        return move(value, lambda z, y, x, c: (z ^ 1 if x else z, y, x, c))

    def last_forward_cross(value):
        return move(value, lambda z, y, x, c: (z if x else z ^ 1, y, 1 - x, c))

    def near_left(value):
        return move(value, lambda z, y, x, c: (z, 1 - y, x, c) if c == y else (z, y, x, 1 - c))

    def far_left(value):
        return move(value, lambda z, y, x, c: (z, y, x, c) if c == y else (z, 1 - y, x, 1 - c))

    vmem = pl.BlockSpec(memory_space=pltpu.VMEM)
    unread = pl.BlockSpec(memory_space=pl.ANY)
    params = pltpu.CompilerParams(vmem_limit_bytes=VMEM_LIMIT)

    def shape(dtype, *dims):
        return jax.ShapeDtypeStruct(dims, dtype)

    def call(name, kernel, outs, operands, earlier=(), scratch=(), flops=0):
        many = isinstance(outs, list)
        with jax.named_scope(name):
            return pl.pallas_call(
                kernel,
                in_specs=[vmem] * len(operands) + [unread] * len(earlier),
                out_specs=[vmem] * len(outs) if many else vmem,
                out_shape=outs,
                scratch_shapes=list(scratch),
                compiler_params=params,
                cost_estimate=pl.CostEstimate(
                    flops=flops,
                    bytes_accessed=0,
                    transcendentals=0,
                ),
            )(*operands, *earlier)

    metric_high, metric_low = call(
        "metric_turn",
        turn_metric_kernel,
        [shape(jnp.bfloat16, n_sec, width, aux_total)] * 2,
        [metric],
        flops=4 * aux_total * aux_total * width,
    )
    with jax.named_scope("gather"):
        swapped, opposite, metric_high = lax.optimization_barrier(
            (
                x_swap(own),
                opposite_layer(own),
                metric_high,
            )
        )
        last_swapped, last_own, first_own, first_cross, near_own, far_own = lax.optimization_barrier(
            (
                last_forward_cross(opposite),
                last_forward(opposite),
                first_partner(own),
                first_partner_cross(own),
                near_left(own),
                far_left(own),
            )
        )
        near_swapped = near_left(swapped)
        far_swapped = far_left(swapped)
        left = [own, swapped, near_own, near_swapped, far_own, far_swapped]
        first = [first_own, first_cross, core_swap(first_own), core_swap(first_cross)]
        last = [last_own, last_swapped, core_swap(last_own), core_swap(last_swapped)]

    energies = [occ_energy[None, :], vir_energy[None, :]]
    first_half, last_half = call(
        "half_overlap",
        half_overlap_kernel,
        [shape(jnp.float32, virtuals, virtuals)] * 2,
        [*left[:4], *first[:2], *last[:2]],
        flops=2 * square * aux_total,
    )
    half_square = shape(jnp.bfloat16, virtuals, virtuals)
    grad, first_amp, first_mixed = call(
        "first_pair",
        first_pair_kernel,
        [shape(jnp.float32, virtuals, aux_total), half_square, half_square],
        [*energies, first_half, *left[2:], *first],
    )
    last_amp, last_mixed = call(
        "last_pair",
        last_pair_kernel,
        [half_square, half_square],
        [*energies, last_half, *left[2:], *last[2:]],
        [first_amp],
        flops=4 * square * aux_total,
    )
    layers = n_blk // 2
    dens_keep, dens_send = call(
        "density_pairs",
        density_pairs_kernel,
        [shape(jnp.float32, layers, rows, virtuals)] * 2,
        [first_amp, first_mixed, last_amp, last_mixed],
        flops=2 * square * virtuals,
    )
    dens_got = core_swap(dens_send)

    message = shape(jnp.bfloat16, width + TAIL_ROWS, virtuals)
    block_flops = 6 * width * virtuals * aux_total
    high, low, third = call(
        "gradient",
        functools.partial(gradient_kernel, 3),
        [
            shape(jnp.bfloat16, virtuals, aux_total),
            shape(jnp.bfloat16, virtuals, aux_total),
            message,
        ],
        [last_mixed, *last, grad, metric_high, metric_low],
        flops=2 * block_flops,
    )

    def gamma_block(step, *earlier):
        return call(
            "gamma_block",
            functools.partial(metric_kernel, step),
            message,
            [metric_high, metric_low, high, low],
            earlier,
            flops=block_flops,
        )

    def gamma_move(step, block):
        return move(block, lambda z, y, x, c: (z, c, x ^ (step >> 1), y ^ (step & 1)))

    def across(value):
        return move(value, lambda z, y, x, c: (z, 1 - c, 1 - x, y))

    def along(value):
        return move(value, lambda z, y, x, c: (z, 1 - c, x, y))

    coded = shape(jnp.bfloat16, rows + TAIL_ROWS, virtuals)
    got_third = gamma_move(3, third)
    layer, *messages = call(
        "density_cores",
        density_cores_kernel,
        [shape(jnp.float32, rows, virtuals)] + [coded] * (layers - 1),
        [dens_keep, dens_got],
        [third],
    )
    got = [
        move(messages[step - 1], lambda z, y, x, c, step=step: (z ^ step, y, x, c))
        for step in range(layers - 1, 0, -1)
    ]
    second = gamma_block(2, messages[0])
    got_second = gamma_move(2, second)
    third_part = call(
        "gamma_third",
        decode_kernel,
        shape(jnp.float32, width, virtuals),
        [got_third],
        [second],
    )
    first_block = gamma_block(1, third_part)
    got_first = gamma_move(1, first_block)
    partial_rows = call(
        "density_rows",
        density_rows_kernel,
        coded,
        [layer, *got],
        [first_block],
    )
    rows_far, rows_near = across(partial_rows), along(partial_rows)
    zeroth = gamma_block(0, partial_rows)
    got_zeroth = gamma_move(0, zeroth)
    part = call(
        "gamma_part",
        gamma_part_kernel,
        shape(jnp.float32, width, virtuals),
        [third_part, got_second],
        [zeroth, partial_rows],
    )
    block = call(
        "density_block",
        density_block_kernel,
        shape(jnp.float32, rows, virtuals),
        [rows_far, rows_near],
        [part],
    )
    other = core_swap(block)
    gamma = call(
        "gamma_sum",
        gamma_sum_kernel,
        shape(jnp.float32, width, 1, virtuals),
        [part, got_first, got_zeroth],
        [block],
    )
    density = call(
        "density_sum",
        density_sum_kernel,
        shape(jnp.float32, rows, virtuals),
        [block, other],
    )
    return gamma, density


def solution(mesh):
    n_blk, n_sec = mesh.shape["blk"], mesh.shape["sec"]

    def per_device(factors, occ_energy, vir_energy, metric):
        two_rows_of_layers = n_sec == 4 and n_blk == 2 * n_sec and factors.shape[0] == 1
        step = fast_device if two_rows_of_layers else general_device
        return step(factors, occ_energy, vir_energy, metric)

    return jax.shard_map(
        per_device,
        mesh=mesh,
        in_specs=(P("blk", None, "sec"), P(), P(), P()),
        out_specs=(P("sec", "blk", None), P("blk", None)),
        check_vma=False,
    )
```

```python
import functools

import jax
import jax.numpy as jnp
from jax import lax
from jax.experimental import pallas as pl
from jax.experimental.pallas import tpu as pltpu
from jax.sharding import PartitionSpec as P

CYCLE_STEPS = 4


def from_behind(shard, axis, by):
    devices = lax.axis_size(axis)
    return lax.ppermute(shard, axis, [(i, (i + by) % devices) for i in range(devices)])


def batch_energy(occ_energy, batch_index, per_batch):
    return lax.dynamic_slice_in_dim(occ_energy, batch_index * per_batch, per_batch, 0)


def pair_block(
    own_full, own_energy, partner, part_energy, vir_energy, acc_own, acc_part, density, weight
):
    per_batch = own_full.shape[0]

    def one_pair(pair_index, loop_state):
        acc_own, acc_part, density = loop_state
        first_pos = pair_index // per_batch
        second = pair_index % per_batch
        left_block = lax.dynamic_index_in_dim(own_full, first_pos, 0, keepdims=False)
        right_block = lax.dynamic_index_in_dim(partner, second, 0, keepdims=False)
        intersection = lax.dot_general(
            left_block, right_block, (((1,), (1,)), ((), ())), preferred_element_type=jnp.float32
        )
        energy_sum = lax.dynamic_index_in_dim(
            own_energy, first_pos, 0, keepdims=False
        ) + lax.dynamic_index_in_dim(part_energy, second, 0, keepdims=False)
        denominator = energy_sum - vir_energy[:, None] - vir_energy[None, :]
        amplitude = intersection / denominator
        mixed_amp = 2.0 * amplitude - amplitude.T
        amp_half = amplitude.astype(jnp.bfloat16)
        mixed_half = mixed_amp.astype(jnp.bfloat16)
        own_term = jnp.einsum(
            "bp,ab->pa", right_block, mixed_half, preferred_element_type=jnp.float32
        )
        acc_own = acc_own.at[first_pos].add(weight * own_term)
        dens_term = lax.dot_general(
            mixed_half, amp_half, (((1,), (1,)), ((), ())), preferred_element_type=jnp.float32
        )
        part_term = jnp.einsum(
            "ap,ab->pb", left_block, mixed_half, preferred_element_type=jnp.float32
        )
        acc_part = acc_part.at[second].add(weight * part_term)
        dens_term = dens_term + lax.dot_general(
            mixed_half, amp_half, (((0,), (0,)), ((), ())), preferred_element_type=jnp.float32
        )
        density = density + weight * dens_term
        return (acc_own, acc_part, density)

    return lax.fori_loop(0, per_batch * per_batch, one_pair, (acc_own, acc_part, density))


def general_device(factors, occ_energy, vir_energy, metric):
    n_blk = lax.axis_size("blk")
    n_sec = lax.axis_size("sec")
    blk_pos = lax.axis_index("blk")
    sec_pos = lax.axis_index("sec")
    per_batch = factors.shape[0]
    virtuals = factors.shape[1]
    aux_part = factors.shape[2]
    aux_total = aux_part * n_sec
    cycle_turns = min(CYCLE_STEPS, n_blk // (2 * n_sec))
    own_full = lax.all_gather(factors, "sec", axis=2, tiled=True)
    own_energy = batch_energy(occ_energy, blk_pos, per_batch)
    acc_own = jnp.zeros((per_batch, aux_total, virtuals), jnp.float32)
    density = jnp.zeros((virtuals, virtuals), jnp.float32)
    segmented = [factors]
    moving = factors
    for shift_turn in range(n_sec - 1):
        moving = from_behind(moving, "blk", 1)
        segmented.append(moving)
    partner = lax.all_to_all(
        jnp.stack(segmented, 0), "sec", split_axis=0, concat_axis=3, tiled=True
    )[0]
    acc_part = jnp.zeros((per_batch, aux_total, virtuals), jnp.float32)
    for cycle_step in range(cycle_turns):
        if cycle_step > 0:
            partner = from_behind(partner, "blk", n_sec)
            acc_part = from_behind(acc_part, "blk", n_sec)
        offset = sec_pos + n_sec * cycle_step
        weight = jnp.where(offset == 0, jnp.float32(0.5), jnp.float32(1.0))
        part_energy = batch_energy(occ_energy, (blk_pos - offset) % n_blk, per_batch)
        acc_own, acc_part, density = pair_block(
            own_full,
            own_energy,
            partner,
            part_energy,
            vir_energy,
            acc_own,
            acc_part,
            density,
            weight,
        )
    if cycle_turns > 1:
        acc_part = from_behind(acc_part, "blk", -n_sec * (cycle_turns - 1))
    regrouped = lax.all_to_all(acc_part[None], "sec", split_axis=2, concat_axis=0, tiled=True)
    carried = regrouped[n_sec - 1]
    for shift_turn in range(n_sec - 2, -1, -1):
        carried = from_behind(carried, "blk", -1) + regrouped[shift_turn]
    metric_rows = lax.dynamic_slice_in_dim(metric, sec_pos * aux_part, aux_part, 0)
    own_term = jnp.einsum("pq,ipa->qia", metric, acc_own, precision=lax.Precision.HIGHEST)
    gamma_part = lax.psum_scatter(
        own_term + jnp.einsum("pq,ipa->qia", metric_rows, carried, precision=lax.Precision.HIGHEST),
        "sec",
        scatter_dimension=0,
        tiled=True,
    )
    density_rows = lax.psum_scatter(density, "blk", scatter_dimension=0, tiled=True)
    density_out = lax.psum(density_rows, "sec")
    return (gamma_part, density_out)


AXES = ("blk", "sec")
NT = (((1,), (1,)), ((), ()))
NN = (((1,), (0,)), ((), ()))
TAIL_ROWS = 16
VMEM_LIMIT = 16 * 1024 * 1024


def dot(left, right, dims):
    return lax.dot_general(left, right, dims, preferred_element_type=jnp.float32)


def split_bits(device, n_sec):
    blk, sec = device // n_sec, device % n_sec
    return blk // 2, blk % 2, sec // 2, sec % 2


def join_bits(z, y, x, c, n_sec):
    return (2 * z + y) * n_sec + 2 * x + c


def send(value, target, n_blk, n_sec):
    pairs = []
    for device in range(n_blk * n_sec):
        pairs.append((device, join_bits(*target(*split_bits(device, n_sec)), n_sec)))
    return lax.ppermute(value, AXES, pairs)


def encode(value):
    peak = jnp.max(jnp.abs(value), keepdims=True)
    power = jnp.floor(15.4 - jnp.log2(jnp.maximum(peak, 1e-36)))
    power = jnp.clip(power, -120.0, 120.0)
    scaled = value * jnp.exp2(power)
    second = scaled * scaled
    fourth = second * second
    eighth = fourth * fourth
    coded = jnp.where(scaled < 0.0, -eighth, eighth).astype(jnp.bfloat16)
    tail = jnp.broadcast_to(power, (TAIL_ROWS, value.shape[1])).astype(jnp.bfloat16)
    return coded, tail


def encode_into(out, value):
    rows = value.shape[0]
    coded, tail = encode(value)
    out[:rows] = coded
    out[rows:] = tail


def decode(ref):
    rows = ref.shape[0] - TAIL_ROWS
    power = ref[rows:].astype(jnp.float32)[:1]
    coded = ref[:rows].astype(jnp.float32)
    root = jnp.exp2(jnp.log2(jnp.abs(coded)) * 0.125 - power)
    return jnp.where(coded < 0.0, -root, root)


def place_bits():
    blk, sec = lax.axis_index("blk"), lax.axis_index("sec")
    return blk // 2, blk % 2, sec // 2, sec % 2


def pair_terms(occupied, virtual, layer, overlap):
    z, y, x, c = place_bits()
    index = lax.broadcasted_iota(jnp.int32, occupied.shape, 1)

    def energy(batch):
        return jnp.sum(jnp.where(index == batch, occupied[...], 0.0), axis=1, keepdims=True)

    row_energy = virtual[...]
    row_sum = energy(2 * z + c) + energy(2 * layer + y) - row_energy
    col_sum = jnp.broadcast_to(row_sum, (128, row_sum.shape[1])).T[:, :1]
    amplitude = overlap / (col_sum - row_energy)
    return amplitude.astype(jnp.bfloat16), 2.0 * amplitude - amplitude.T


def half_overlap_kernel(own, swapped, near, near_swapped, *refs):
    z, y, x, c = place_bits()
    home = c == y
    left = jnp.where(home, own[...], near[...])
    left_swapped = jnp.where(home, swapped[...], near_swapped[...])
    for pair in range(2):
        right, right_swapped = refs[2 * pair], refs[2 * pair + 1]
        refs[4 + pair][...] = dot(left, right[...], NT) + dot(left_swapped, right_swapped[...], NT)


def whole_overlap(half, lefts, rights):
    z, y, x, c = place_bits()
    home = c == y
    near, near_swapped, far, far_swapped = [ref[...] for ref in lefts]
    right, right_swapped = [ref[...] for ref in rights]
    left = jnp.where(home, near, far)
    left_swapped = jnp.where(home, near_swapped, far_swapped)
    return half[...] + dot(left, right, NT) + dot(left_swapped, right_swapped, NT)


def first_pair_kernel(occupied, virtual, half, *refs):
    z, y, x, c = place_bits()
    overlap = whole_overlap(half, refs[:4], refs[6:8])
    grad_out, amp_out, mixed_out = refs[-3:]
    layer = jnp.where(x == 1, z, z ^ 1)
    amp_half, mixed = pair_terms(occupied, virtual, layer, overlap)
    mixed_half = mixed.astype(jnp.bfloat16)
    width = refs[4].shape[1]
    for part, right in enumerate(refs[4:8]):
        grad_out[:, part * width : (part + 1) * width] = dot(mixed_half, right[...], NN)
    amp_out[...] = amp_half
    mixed_out[...] = mixed_half


def last_pair_kernel(occupied, virtual, half, *refs):
    z, y, x, c = place_bits()
    overlap = whole_overlap(half, refs[:4], refs[4:6])
    amp_out, mixed_out = refs[-2:]
    layer = jnp.where(x == 1, z ^ 3, z ^ 2)
    amp_half, mixed = pair_terms(occupied, virtual, layer, overlap)
    outside = (x == 0) & (c == y)
    amp_out[...] = amp_half
    mixed_out[...] = jnp.where(outside, 0.0, mixed).astype(jnp.bfloat16)


def density_pairs_kernel(first_amp, first_mixed, last_amp, last_mixed, keep_out, send_out):
    z, y, x, c = place_bits()
    count, rows = keep_out.shape[:2]
    for out, core in ((send_out, c), (keep_out, 1 - c)):
        groups = [
            pl.ds(pl.multiple_of((2 * layer + core) * rows, rows), rows) for layer in range(count)
        ]
        first = jnp.concatenate([first_mixed[group, :] for group in groups], 0)
        last = jnp.concatenate([last_mixed[group, :] for group in groups], 0)
        total = dot(first, first_amp[...], NT) + dot(last, last_amp[...], NT)
        for layer in range(count):
            out[layer] = total[layer * rows : (layer + 1) * rows]


def metric_product(step, metric_high, metric_low, high, low):
    metric_top = metric_high[step]
    block = dot(metric_top, high[...], NT)
    block += dot(metric_top, low[...], NT)
    return block + dot(metric_low[step], high[...], NT)


def gradient_kernel(step, mixed, *refs):
    grad_in, metric_high, metric_low, high_out, low_out, out = refs[4:]
    mixed_half = mixed[...]
    width = refs[0].shape[1]
    for part in range(4):
        cols = slice(part * width, (part + 1) * width)
        grad = grad_in[:, cols] + dot(mixed_half, refs[part][...], NN)
        high = grad.astype(jnp.bfloat16)
        high_out[:, cols] = high
        low_out[:, cols] = (grad - high.astype(jnp.float32)).astype(jnp.bfloat16)
    encode_into(out, metric_product(step, metric_high, metric_low, high_out, low_out))


def metric_kernel(step, metric_high, metric_low, high, low, *refs):
    encode_into(refs[-1], metric_product(step, metric_high, metric_low, high, low))


def turn_metric_kernel(metric, *refs):
    high, low = refs[-2:]
    z, y, x, c = place_bits()
    steps, width, aux_total = high.shape
    row = lax.broadcasted_iota(jnp.int32, (width, width), 0)
    col = lax.broadcasted_iota(jnp.int32, (width, width), 1)
    unit = jnp.where(row == col, 1.0, 0.0).astype(jnp.bfloat16)
    lane = 2 * x + c
    for step in range(steps):
        target = 2 * (x ^ (step >> 1)) + (y ^ (step & 1))
        for part, order in enumerate((lane, lane ^ 2, lane ^ 1, lane ^ 3)):
            value = metric[
                pl.ds(pl.multiple_of(order * width, width), width),
                pl.ds(pl.multiple_of(target * width, width), width),
            ]
            top = value.astype(jnp.bfloat16)
            rest = (value - top.astype(jnp.float32)).astype(jnp.bfloat16)
            cols = slice(part * width, (part + 1) * width)
            high[step, :, cols] = dot(unit, top, NT).astype(jnp.bfloat16)
            low[step, :, cols] = dot(unit, rest, NT).astype(jnp.bfloat16)


def decode_kernel(message, *refs):
    refs[-1][...] = decode(message)


def gamma_part_kernel(part, message, *refs):
    refs[-1][...] = part[...] + decode(message)


def density_cores_kernel(keep, got, *refs):
    z, y, x, c = place_bits()
    for step, out in enumerate(refs[-keep.shape[0] :]):
        encode_into(out, keep[z ^ step] + got[z ^ step])


def density_rows_kernel(here, one, two, three, *refs):
    encode_into(refs[-1], decode(here) + decode(one) + decode(two) + decode(three))


def density_block_kernel(far, near, *refs):
    refs[-1][...] = decode(far) + decode(near)


def gamma_sum_kernel(part, left, right, *refs):
    refs[-1][:, 0, :] = part[...] + decode(left) + decode(right)


def density_sum_kernel(block, other, *refs):
    refs[-1][...] = block[...] + other[...]


def fast_device(factors, occ_energy, vir_energy, metric):
    n_blk = lax.axis_size("blk")
    n_sec = lax.axis_size("sec")
    own = factors[0]
    virtuals, width = own.shape
    aux_total = width * n_sec
    half = virtuals // 2
    rows = virtuals // n_blk
    square = 2 * virtuals * virtuals

    def move(value, target):
        return send(value, target, n_blk, n_sec)

    def core_swap(value):
        return move(value, lambda z, y, x, c: (z, y, x, 1 - c))

    def x_swap(value):
        return move(value, lambda z, y, x, c: (z, y, 1 - x, c))

    def y_swap(value):
        return move(value, lambda z, y, x, c: (z, 1 - y, x, c))

    def xy_swap(value):
        return move(value, lambda z, y, x, c: (z, 1 - y, 1 - x, c))

    def first_partner(value):
        return move(value, lambda z, y, x, c: (z if x else z ^ 1, y, x, c))

    def first_partner_cross(value):
        return move(value, lambda z, y, x, c: (z ^ 1 if x else z, y, 1 - x, c))

    def opposite_layer(value):
        return move(value, lambda z, y, x, c: (z ^ 2, y, x, c))

    def last_forward(value):
        return move(value, lambda z, y, x, c: (z ^ 1 if x else z, y, x, c))

    def last_forward_cross(value):
        return move(value, lambda z, y, x, c: (z if x else z ^ 1, y, 1 - x, c))

    def near_left(value):
        return move(value, lambda z, y, x, c: (z, 1 - y, x, c) if c == y else (z, y, x, 1 - c))

    def far_left(value):
        return move(value, lambda z, y, x, c: (z, y, x, c) if c == y else (z, 1 - y, x, 1 - c))

    vmem = pl.BlockSpec(memory_space=pltpu.VMEM)
    unread = pl.BlockSpec(memory_space=pl.ANY)
    params = pltpu.CompilerParams(vmem_limit_bytes=VMEM_LIMIT)

    def shape(dtype, *dims):
        return jax.ShapeDtypeStruct(dims, dtype)

    def call(name, kernel, outs, operands, earlier=(), scratch=(), flops=0):
        many = isinstance(outs, list)
        with jax.named_scope(name):
            return pl.pallas_call(
                kernel,
                in_specs=[vmem] * len(operands) + [unread] * len(earlier),
                out_specs=[vmem] * len(outs) if many else vmem,
                out_shape=outs,
                scratch_shapes=list(scratch),
                compiler_params=params,
                cost_estimate=pl.CostEstimate(
                    flops=flops,
                    bytes_accessed=0,
                    transcendentals=0,
                ),
            )(*operands, *earlier)

    metric_high, metric_low = call(
        "metric_turn",
        turn_metric_kernel,
        [shape(jnp.bfloat16, n_sec, width, aux_total)] * 2,
        [metric],
        flops=4 * aux_total * aux_total * width,
    )
    with jax.named_scope("gather"):
        swapped, opposite, metric_high = lax.optimization_barrier(
            (
                x_swap(own),
                opposite_layer(own),
                metric_high,
            )
        )
        last_swapped, last_own, first_own, first_cross, near_own, far_own = lax.optimization_barrier(
            (
                last_forward_cross(opposite),
                last_forward(opposite),
                first_partner(own),
                first_partner_cross(own),
                near_left(own),
                far_left(own),
            )
        )
        near_swapped = near_left(swapped)
        far_swapped = far_left(swapped)
        left = [own, swapped, near_own, near_swapped, far_own, far_swapped]
        first = [first_own, first_cross, core_swap(first_own), core_swap(first_cross)]
        last = [last_own, last_swapped, core_swap(last_own), core_swap(last_swapped)]

    energies = [occ_energy[None, :], vir_energy[None, :]]
    first_half, last_half = call(
        "half_overlap",
        half_overlap_kernel,
        [shape(jnp.float32, virtuals, virtuals)] * 2,
        [*left[:4], *first[:2], *last[:2]],
        flops=2 * square * aux_total,
    )
    half_square = shape(jnp.bfloat16, virtuals, virtuals)
    grad, first_amp, first_mixed = call(
        "first_pair",
        first_pair_kernel,
        [shape(jnp.float32, virtuals, aux_total), half_square, half_square],
        [*energies, first_half, *left[2:], *first],
    )
    last_amp, last_mixed = call(
        "last_pair",
        last_pair_kernel,
        [half_square, half_square],
        [*energies, last_half, *left[2:], *last[2:]],
        [first_amp],
        flops=4 * square * aux_total,
    )
    layers = n_blk // 2
    dens_keep, dens_send = call(
        "density_pairs",
        density_pairs_kernel,
        [shape(jnp.float32, layers, rows, virtuals)] * 2,
        [first_amp, first_mixed, last_amp, last_mixed],
        flops=2 * square * virtuals,
    )
    dens_got = core_swap(dens_send)

    message = shape(jnp.bfloat16, width + TAIL_ROWS, virtuals)
    block_flops = 6 * width * virtuals * aux_total
    high, low, third = call(
        "gradient",
        functools.partial(gradient_kernel, 3),
        [
            shape(jnp.bfloat16, virtuals, aux_total),
            shape(jnp.bfloat16, virtuals, aux_total),
            message,
        ],
        [last_mixed, *last, grad, metric_high, metric_low],
        flops=2 * block_flops,
    )

    def gamma_block(step, *earlier):
        return call(
            "gamma_block",
            functools.partial(metric_kernel, step),
            message,
            [metric_high, metric_low, high, low],
            earlier,
            flops=block_flops,
        )

    def gamma_move(step, block):
        return move(block, lambda z, y, x, c: (z, c, x ^ (step >> 1), y ^ (step & 1)))

    def to_rows(step, value):
        return move(value, lambda z, y, x, c: (z ^ step, 1 - c, x, y))

    coded = shape(jnp.bfloat16, rows + TAIL_ROWS, virtuals)
    got_third = gamma_move(3, third)
    messages = call(
        "density_cores",
        density_cores_kernel,
        [coded] * layers,
        [dens_keep, dens_got],
        [third],
    )
    got = [to_rows(step, messages[step]) for step in range(layers - 1, -1, -1)]
    second = gamma_block(2, messages[0])
    got_second = gamma_move(2, second)
    third_part = call(
        "gamma_third",
        decode_kernel,
        shape(jnp.float32, width, virtuals),
        [got_third],
        [second],
    )
    first_block = gamma_block(1, third_part)
    got_first = gamma_move(1, first_block)
    partial_rows = call(
        "density_rows",
        density_rows_kernel,
        coded,
        got,
        [first_block],
    )
    rows_got = x_swap(partial_rows)
    zeroth = gamma_block(0, partial_rows)
    got_zeroth = gamma_move(0, zeroth)
    part = call(
        "gamma_part",
        gamma_part_kernel,
        shape(jnp.float32, width, virtuals),
        [third_part, got_second],
        [zeroth, partial_rows],
    )
    block = call(
        "density_block",
        density_block_kernel,
        shape(jnp.float32, rows, virtuals),
        [partial_rows, rows_got],
        [part],
    )
    other = core_swap(block)
    gamma = call(
        "gamma_sum",
        gamma_sum_kernel,
        shape(jnp.float32, width, 1, virtuals),
        [part, got_first, got_zeroth],
        [block],
    )
    density = call(
        "density_sum",
        density_sum_kernel,
        shape(jnp.float32, rows, virtuals),
        [block, other],
    )
    return gamma, density


def solution(mesh):
    n_blk, n_sec = mesh.shape["blk"], mesh.shape["sec"]

    def per_device(factors, occ_energy, vir_energy, metric):
        two_rows_of_layers = n_sec == 4 and n_blk == 2 * n_sec and factors.shape[0] == 1
        step = fast_device if two_rows_of_layers else general_device
        return step(factors, occ_energy, vir_energy, metric)

    return jax.shard_map(
        per_device,
        mesh=mesh,
        in_specs=(P("blk", None, "sec"), P(), P(), P()),
        out_specs=(P("sec", "blk", None), P("blk", None)),
        check_vma=False,
    )
```

```python
import functools

import jax
import jax.numpy as jnp
from jax import lax
from jax.experimental import pallas as pl
from jax.experimental.pallas import tpu as pltpu
from jax.sharding import PartitionSpec as P

CYCLE_STEPS = 4


def from_behind(shard, axis, by):
    devices = lax.axis_size(axis)
    return lax.ppermute(shard, axis, [(i, (i + by) % devices) for i in range(devices)])


def batch_energy(occ_energy, batch_index, per_batch):
    return lax.dynamic_slice_in_dim(occ_energy, batch_index * per_batch, per_batch, 0)


def pair_block(
    own_full, own_energy, partner, part_energy, vir_energy, acc_own, acc_part, density, weight
):
    per_batch = own_full.shape[0]

    def one_pair(pair_index, loop_state):
        acc_own, acc_part, density = loop_state
        first_pos = pair_index // per_batch
        second = pair_index % per_batch
        left_block = lax.dynamic_index_in_dim(own_full, first_pos, 0, keepdims=False)
        right_block = lax.dynamic_index_in_dim(partner, second, 0, keepdims=False)
        intersection = lax.dot_general(
            left_block, right_block, (((1,), (1,)), ((), ())), preferred_element_type=jnp.float32
        )
        energy_sum = lax.dynamic_index_in_dim(
            own_energy, first_pos, 0, keepdims=False
        ) + lax.dynamic_index_in_dim(part_energy, second, 0, keepdims=False)
        denominator = energy_sum - vir_energy[:, None] - vir_energy[None, :]
        amplitude = intersection / denominator
        mixed_amp = 2.0 * amplitude - amplitude.T
        amp_half = amplitude.astype(jnp.bfloat16)
        mixed_half = mixed_amp.astype(jnp.bfloat16)
        own_term = jnp.einsum(
            "bp,ab->pa", right_block, mixed_half, preferred_element_type=jnp.float32
        )
        acc_own = acc_own.at[first_pos].add(weight * own_term)
        dens_term = lax.dot_general(
            mixed_half, amp_half, (((1,), (1,)), ((), ())), preferred_element_type=jnp.float32
        )
        part_term = jnp.einsum(
            "ap,ab->pb", left_block, mixed_half, preferred_element_type=jnp.float32
        )
        acc_part = acc_part.at[second].add(weight * part_term)
        dens_term = dens_term + lax.dot_general(
            mixed_half, amp_half, (((0,), (0,)), ((), ())), preferred_element_type=jnp.float32
        )
        density = density + weight * dens_term
        return (acc_own, acc_part, density)

    return lax.fori_loop(0, per_batch * per_batch, one_pair, (acc_own, acc_part, density))


def general_device(factors, occ_energy, vir_energy, metric):
    n_blk = lax.axis_size("blk")
    n_sec = lax.axis_size("sec")
    blk_pos = lax.axis_index("blk")
    sec_pos = lax.axis_index("sec")
    per_batch = factors.shape[0]
    virtuals = factors.shape[1]
    aux_part = factors.shape[2]
    aux_total = aux_part * n_sec
    cycle_turns = min(CYCLE_STEPS, n_blk // (2 * n_sec))
    own_full = lax.all_gather(factors, "sec", axis=2, tiled=True)
    own_energy = batch_energy(occ_energy, blk_pos, per_batch)
    acc_own = jnp.zeros((per_batch, aux_total, virtuals), jnp.float32)
    density = jnp.zeros((virtuals, virtuals), jnp.float32)
    segmented = [factors]
    moving = factors
    for shift_turn in range(n_sec - 1):
        moving = from_behind(moving, "blk", 1)
        segmented.append(moving)
    partner = lax.all_to_all(
        jnp.stack(segmented, 0), "sec", split_axis=0, concat_axis=3, tiled=True
    )[0]
    acc_part = jnp.zeros((per_batch, aux_total, virtuals), jnp.float32)
    for cycle_step in range(cycle_turns):
        if cycle_step > 0:
            partner = from_behind(partner, "blk", n_sec)
            acc_part = from_behind(acc_part, "blk", n_sec)
        offset = sec_pos + n_sec * cycle_step
        weight = jnp.where(offset == 0, jnp.float32(0.5), jnp.float32(1.0))
        part_energy = batch_energy(occ_energy, (blk_pos - offset) % n_blk, per_batch)
        acc_own, acc_part, density = pair_block(
            own_full,
            own_energy,
            partner,
            part_energy,
            vir_energy,
            acc_own,
            acc_part,
            density,
            weight,
        )
    if cycle_turns > 1:
        acc_part = from_behind(acc_part, "blk", -n_sec * (cycle_turns - 1))
    regrouped = lax.all_to_all(acc_part[None], "sec", split_axis=2, concat_axis=0, tiled=True)
    carried = regrouped[n_sec - 1]
    for shift_turn in range(n_sec - 2, -1, -1):
        carried = from_behind(carried, "blk", -1) + regrouped[shift_turn]
    metric_rows = lax.dynamic_slice_in_dim(metric, sec_pos * aux_part, aux_part, 0)
    own_term = jnp.einsum("pq,ipa->qia", metric, acc_own, precision=lax.Precision.HIGHEST)
    gamma_part = lax.psum_scatter(
        own_term + jnp.einsum("pq,ipa->qia", metric_rows, carried, precision=lax.Precision.HIGHEST),
        "sec",
        scatter_dimension=0,
        tiled=True,
    )
    density_rows = lax.psum_scatter(density, "blk", scatter_dimension=0, tiled=True)
    density_out = lax.psum(density_rows, "sec")
    return (gamma_part, density_out)


AXES = ("blk", "sec")
NT = (((1,), (1,)), ((), ()))
NN = (((1,), (0,)), ((), ()))
TAIL_ROWS = 16
VMEM_LIMIT = 16 * 1024 * 1024


def dot(left, right, dims):
    return lax.dot_general(left, right, dims, preferred_element_type=jnp.float32)


def split_bits(device, n_sec):
    blk, sec = device // n_sec, device % n_sec
    return blk // 2, blk % 2, sec // 2, sec % 2


def join_bits(z, y, x, c, n_sec):
    return (2 * z + y) * n_sec + 2 * x + c


def send(value, target, n_blk, n_sec):
    pairs = []
    for device in range(n_blk * n_sec):
        pairs.append((device, join_bits(*target(*split_bits(device, n_sec)), n_sec)))
    return lax.ppermute(value, AXES, pairs)


def encode(value):
    peak = jnp.max(jnp.abs(value), keepdims=True)
    power = jnp.floor(15.4 - jnp.log2(jnp.maximum(peak, 1e-36)))
    power = jnp.clip(power, -120.0, 120.0)
    scaled = value * jnp.exp2(power)
    second = scaled * scaled
    coded = ((second * second) * (second * scaled)).astype(jnp.bfloat16)
    tail = jnp.broadcast_to(power, (TAIL_ROWS, value.shape[1])).astype(jnp.bfloat16)
    return coded, tail


def encode_into(out, value):
    rows = value.shape[0]
    coded, tail = encode(value)
    out[:rows] = coded
    out[rows:] = tail


def decode(ref):
    rows = ref.shape[0] - TAIL_ROWS
    power = ref[rows:].astype(jnp.float32)[:1]
    coded = ref[:rows].astype(jnp.float32)
    root = jnp.exp2(jnp.log2(jnp.abs(coded)) * (1.0 / 7.0) - power)
    return jnp.where(coded < 0.0, -root, root)


def place_bits():
    blk, sec = lax.axis_index("blk"), lax.axis_index("sec")
    return blk // 2, blk % 2, sec // 2, sec % 2


def pair_terms(occupied, virtual, layer, overlap):
    z, y, x, c = place_bits()
    index = lax.broadcasted_iota(jnp.int32, occupied.shape, 1)

    def energy(batch):
        return jnp.sum(jnp.where(index == batch, occupied[...], 0.0), axis=1, keepdims=True)

    row_energy = virtual[...]
    row_sum = energy(2 * z + c) + energy(2 * layer + y) - row_energy
    col_sum = jnp.broadcast_to(row_sum, (128, row_sum.shape[1])).T[:, :1]
    amplitude = overlap / (col_sum - row_energy)
    return amplitude.astype(jnp.bfloat16), 2.0 * amplitude - amplitude.T


def half_overlap_kernel(own, swapped, near, near_swapped, *refs):
    z, y, x, c = place_bits()
    home = c == y
    left = jnp.where(home, own[...], near[...])
    left_swapped = jnp.where(home, swapped[...], near_swapped[...])
    for pair in range(2):
        right, right_swapped = refs[2 * pair], refs[2 * pair + 1]
        refs[4 + pair][...] = dot(left, right[...], NT) + dot(left_swapped, right_swapped[...], NT)


def whole_overlap(half, lefts, rights):
    z, y, x, c = place_bits()
    home = c == y
    near, near_swapped, far, far_swapped = [ref[...] for ref in lefts]
    right, right_swapped = [ref[...] for ref in rights]
    left = jnp.where(home, near, far)
    left_swapped = jnp.where(home, near_swapped, far_swapped)
    return half[...] + dot(left, right, NT) + dot(left_swapped, right_swapped, NT)


def first_pair_kernel(occupied, virtual, half, *refs):
    z, y, x, c = place_bits()
    overlap = whole_overlap(half, refs[:4], refs[6:8])
    grad_out, amp_out, mixed_out = refs[-3:]
    layer = jnp.where(x == 1, z, z ^ 1)
    amp_half, mixed = pair_terms(occupied, virtual, layer, overlap)
    mixed_half = mixed.astype(jnp.bfloat16)
    width = refs[4].shape[1]
    for part, right in enumerate(refs[4:8]):
        grad_out[:, part * width : (part + 1) * width] = dot(mixed_half, right[...], NN)
    amp_out[...] = amp_half
    mixed_out[...] = mixed_half


def last_pair_kernel(occupied, virtual, half, *refs):
    z, y, x, c = place_bits()
    overlap = whole_overlap(half, refs[:4], refs[4:6])
    amp_out, mixed_out = refs[-2:]
    layer = jnp.where(x == 1, z ^ 3, z ^ 2)
    amp_half, mixed = pair_terms(occupied, virtual, layer, overlap)
    outside = (x == 0) & (c == y)
    amp_out[...] = amp_half
    mixed_out[...] = jnp.where(outside, 0.0, mixed).astype(jnp.bfloat16)


def density_pairs_kernel(first_amp, first_mixed, last_amp, last_mixed, keep_out, send_out):
    z, y, x, c = place_bits()
    count, rows = keep_out.shape[:2]
    for out, core in ((send_out, c), (keep_out, 1 - c)):
        groups = [
            pl.ds(pl.multiple_of((2 * layer + core) * rows, rows), rows) for layer in range(count)
        ]
        first = jnp.concatenate([first_mixed[group, :] for group in groups], 0)
        last = jnp.concatenate([last_mixed[group, :] for group in groups], 0)
        total = dot(first, first_amp[...], NT) + dot(last, last_amp[...], NT)
        for layer in range(count):
            out[layer] = total[layer * rows : (layer + 1) * rows]


def metric_product(step, metric_high, metric_low, high, low):
    metric_top = metric_high[step]
    block = dot(metric_top, high[...], NT)
    block += dot(metric_top, low[...], NT)
    return block + dot(metric_low[step], high[...], NT)


def gradient_kernel(step, mixed, *refs):
    grad_in, metric_high, metric_low, high_out, low_out, out = refs[4:]
    mixed_half = mixed[...]
    width = refs[0].shape[1]
    for part in range(4):
        cols = slice(part * width, (part + 1) * width)
        grad = grad_in[:, cols] + dot(mixed_half, refs[part][...], NN)
        high = grad.astype(jnp.bfloat16)
        high_out[:, cols] = high
        low_out[:, cols] = (grad - high.astype(jnp.float32)).astype(jnp.bfloat16)
    encode_into(out, metric_product(step, metric_high, metric_low, high_out, low_out))


def metric_kernel(step, metric_high, metric_low, high, low, *refs):
    encode_into(refs[-1], metric_product(step, metric_high, metric_low, high, low))


def turn_metric_kernel(metric, *refs):
    high, low = refs[-2:]
    z, y, x, c = place_bits()
    steps, width, aux_total = high.shape
    row = lax.broadcasted_iota(jnp.int32, (width, width), 0)
    col = lax.broadcasted_iota(jnp.int32, (width, width), 1)
    unit = jnp.where(row == col, 1.0, 0.0).astype(jnp.bfloat16)
    lane = 2 * x + c
    for step in range(steps):
        target = 2 * (x ^ (step >> 1)) + (y ^ (step & 1))
        for part, order in enumerate((lane, lane ^ 2, lane ^ 1, lane ^ 3)):
            value = metric[
                pl.ds(pl.multiple_of(order * width, width), width),
                pl.ds(pl.multiple_of(target * width, width), width),
            ]
            top = value.astype(jnp.bfloat16)
            rest = (value - top.astype(jnp.float32)).astype(jnp.bfloat16)
            cols = slice(part * width, (part + 1) * width)
            high[step, :, cols] = dot(unit, top, NT).astype(jnp.bfloat16)
            low[step, :, cols] = dot(unit, rest, NT).astype(jnp.bfloat16)


def decode_kernel(message, *refs):
    refs[-1][...] = decode(message)


def gamma_part_kernel(part, message, *refs):
    refs[-1][...] = part[...] + decode(message)


def density_cores_kernel(keep, got, *refs):
    z, y, x, c = place_bits()
    for step, out in enumerate(refs[-keep.shape[0] :]):
        encode_into(out, keep[z ^ step] + got[z ^ step])


def density_rows_kernel(here, one, two, three, *refs):
    encode_into(refs[-1], decode(here) + decode(one) + decode(two) + decode(three))


def density_block_kernel(far, near, *refs):
    refs[-1][...] = decode(far) + decode(near)


def gamma_sum_kernel(part, left, right, *refs):
    refs[-1][:, 0, :] = part[...] + decode(left) + decode(right)


def density_sum_kernel(block, other, *refs):
    refs[-1][...] = block[...] + other[...]


def fast_device(factors, occ_energy, vir_energy, metric):
    n_blk = lax.axis_size("blk")
    n_sec = lax.axis_size("sec")
    own = factors[0]
    virtuals, width = own.shape
    aux_total = width * n_sec
    half = virtuals // 2
    rows = virtuals // n_blk
    square = 2 * virtuals * virtuals

    def move(value, target):
        return send(value, target, n_blk, n_sec)

    def core_swap(value):
        return move(value, lambda z, y, x, c: (z, y, x, 1 - c))

    def x_swap(value):
        return move(value, lambda z, y, x, c: (z, y, 1 - x, c))

    def y_swap(value):
        return move(value, lambda z, y, x, c: (z, 1 - y, x, c))

    def xy_swap(value):
        return move(value, lambda z, y, x, c: (z, 1 - y, 1 - x, c))

    def first_partner(value):
        return move(value, lambda z, y, x, c: (z if x else z ^ 1, y, x, c))

    def first_partner_cross(value):
        return move(value, lambda z, y, x, c: (z ^ 1 if x else z, y, 1 - x, c))

    def opposite_layer(value):
        return move(value, lambda z, y, x, c: (z ^ 2, y, x, c))

    def last_forward(value):
        return move(value, lambda z, y, x, c: (z ^ 1 if x else z, y, x, c))

    def last_forward_cross(value):
        return move(value, lambda z, y, x, c: (z if x else z ^ 1, y, 1 - x, c))

    def near_left(value):
        return move(value, lambda z, y, x, c: (z, 1 - y, x, c) if c == y else (z, y, x, 1 - c))

    def far_left(value):
        return move(value, lambda z, y, x, c: (z, y, x, c) if c == y else (z, 1 - y, x, 1 - c))

    vmem = pl.BlockSpec(memory_space=pltpu.VMEM)
    unread = pl.BlockSpec(memory_space=pl.ANY)
    params = pltpu.CompilerParams(vmem_limit_bytes=VMEM_LIMIT)

    def shape(dtype, *dims):
        return jax.ShapeDtypeStruct(dims, dtype)

    def call(name, kernel, outs, operands, earlier=(), scratch=(), flops=0):
        many = isinstance(outs, list)
        with jax.named_scope(name):
            return pl.pallas_call(
                kernel,
                in_specs=[vmem] * len(operands) + [unread] * len(earlier),
                out_specs=[vmem] * len(outs) if many else vmem,
                out_shape=outs,
                scratch_shapes=list(scratch),
                compiler_params=params,
                cost_estimate=pl.CostEstimate(
                    flops=flops,
                    bytes_accessed=0,
                    transcendentals=0,
                ),
            )(*operands, *earlier)

    metric_high, metric_low = call(
        "metric_turn",
        turn_metric_kernel,
        [shape(jnp.bfloat16, n_sec, width, aux_total)] * 2,
        [metric],
        flops=4 * aux_total * aux_total * width,
    )
    with jax.named_scope("gather"):
        swapped, opposite, metric_high = lax.optimization_barrier(
            (
                x_swap(own),
                opposite_layer(own),
                metric_high,
            )
        )
        last_swapped, last_own, first_own, first_cross, near_own, far_own = lax.optimization_barrier(
            (
                last_forward_cross(opposite),
                last_forward(opposite),
                first_partner(own),
                first_partner_cross(own),
                near_left(own),
                far_left(own),
            )
        )
        near_swapped = near_left(swapped)
        far_swapped = far_left(swapped)
        left = [own, swapped, near_own, near_swapped, far_own, far_swapped]
        first = [first_own, first_cross, core_swap(first_own), core_swap(first_cross)]
        last = [last_own, last_swapped, core_swap(last_own), core_swap(last_swapped)]

    energies = [occ_energy[None, :], vir_energy[None, :]]
    first_half, last_half = call(
        "half_overlap",
        half_overlap_kernel,
        [shape(jnp.float32, virtuals, virtuals)] * 2,
        [*left[:4], *first[:2], *last[:2]],
        flops=2 * square * aux_total,
    )
    half_square = shape(jnp.bfloat16, virtuals, virtuals)
    grad, first_amp, first_mixed = call(
        "first_pair",
        first_pair_kernel,
        [shape(jnp.float32, virtuals, aux_total), half_square, half_square],
        [*energies, first_half, *left[2:], *first],
    )
    last_amp, last_mixed = call(
        "last_pair",
        last_pair_kernel,
        [half_square, half_square],
        [*energies, last_half, *left[2:], *last[2:]],
        [first_amp],
        flops=4 * square * aux_total,
    )
    layers = n_blk // 2
    dens_keep, dens_send = call(
        "density_pairs",
        density_pairs_kernel,
        [shape(jnp.float32, layers, rows, virtuals)] * 2,
        [first_amp, first_mixed, last_amp, last_mixed],
        flops=2 * square * virtuals,
    )
    dens_got = core_swap(dens_send)

    message = shape(jnp.bfloat16, width + TAIL_ROWS, virtuals)
    block_flops = 6 * width * virtuals * aux_total
    high, low, third = call(
        "gradient",
        functools.partial(gradient_kernel, 3),
        [
            shape(jnp.bfloat16, virtuals, aux_total),
            shape(jnp.bfloat16, virtuals, aux_total),
            message,
        ],
        [last_mixed, *last, grad, metric_high, metric_low],
        flops=2 * block_flops,
    )

    def gamma_block(step, *earlier):
        return call(
            "gamma_block",
            functools.partial(metric_kernel, step),
            message,
            [metric_high, metric_low, high, low],
            earlier,
            flops=block_flops,
        )

    def gamma_move(step, block):
        return move(block, lambda z, y, x, c: (z, c, x ^ (step >> 1), y ^ (step & 1)))

    def to_rows(step, value):
        return move(value, lambda z, y, x, c: (z ^ step, 1 - c, x, y))

    coded = shape(jnp.bfloat16, rows + TAIL_ROWS, virtuals)
    got_third = gamma_move(3, third)
    messages = call(
        "density_cores",
        density_cores_kernel,
        [coded] * layers,
        [dens_keep, dens_got],
        [third],
    )
    got = [to_rows(step, messages[step]) for step in range(layers - 1, -1, -1)]
    second = gamma_block(2, messages[0])
    got_second = gamma_move(2, second)
    third_part = call(
        "gamma_third",
        decode_kernel,
        shape(jnp.float32, width, virtuals),
        [got_third],
        [second],
    )
    first_block = gamma_block(1, third_part)
    got_first = gamma_move(1, first_block)
    partial_rows = call(
        "density_rows",
        density_rows_kernel,
        coded,
        got,
        [first_block],
    )
    rows_got = x_swap(partial_rows)
    zeroth = gamma_block(0, partial_rows)
    got_zeroth = gamma_move(0, zeroth)
    part = call(
        "gamma_part",
        gamma_part_kernel,
        shape(jnp.float32, width, virtuals),
        [third_part, got_second],
        [zeroth, partial_rows],
    )
    block = call(
        "density_block",
        density_block_kernel,
        shape(jnp.float32, rows, virtuals),
        [partial_rows, rows_got],
        [part],
    )
    other = core_swap(block)
    gamma = call(
        "gamma_sum",
        gamma_sum_kernel,
        shape(jnp.float32, width, 1, virtuals),
        [part, got_first, got_zeroth],
        [block],
    )
    density = call(
        "density_sum",
        density_sum_kernel,
        shape(jnp.float32, rows, virtuals),
        [block, other],
    )
    return gamma, density


def solution(mesh):
    n_blk, n_sec = mesh.shape["blk"], mesh.shape["sec"]

    def per_device(factors, occ_energy, vir_energy, metric):
        two_rows_of_layers = n_sec == 4 and n_blk == 2 * n_sec and factors.shape[0] == 1
        step = fast_device if two_rows_of_layers else general_device
        return step(factors, occ_energy, vir_energy, metric)

    return jax.shard_map(
        per_device,
        mesh=mesh,
        in_specs=(P("blk", None, "sec"), P(), P(), P()),
        out_specs=(P("sec", "blk", None), P("blk", None)),
        check_vma=False,
    )
```
